256 devices in a mesh: owner: 16 (over y, x), split: 16 (over z, core).
Axes of the slice: x: 4, y: 4, z: 8, core: 2. Of those that a mesh axis runs over, the one named last changes fastest.
Arguments:
- embeddings: bfloat16 [131072, 1024], P(('owner', 'split'))
- cluster_id: int32 [131072], P(('owner', 'split')), may hold values from 0 to 4095, as said below
- doc_order: int32 [131072], P(('owner', 'split')), may hold values from 0 to 131071, each once
Outputs:
- best_similarity: float32 [131072], P(('owner', 'split'))
The draws below stay inside these ranges and needn't reach their ends.
Inputs may be any that keep to these rules, and one draw needn't show every extreme that they name: `cluster_id`: cluster c belongs to the device with owner index c mod 16 and split index (c // 16) mod 16. Of the rows of one device at most 4 belong to clusters of any one device, and in every draw some device gets exactly 4 rows from every device. The rows of one device hold at most one document of each cluster.
All inputs are finite; a program needn't handle non-finite values.
Results may differ from the reference program's by a relative error of at most 0.00046.
Values may be sent and summed in bfloat16 or wider, within the bound.
A program may use at most 128 MiB of HBM per device.

```python
import math
import jax
import jax.numpy as jnp
from jax import lax

D = 1024
ROWS = 512
OWNERS = 16
SPLITS = 16
DOCS = 131072
CAP = 4
CLUS_DEV = 16
CLUSTERS = 4096


def route_draw(key):
    key = jax.random.fold_in(key, 101)
    key_heavy, key_slots, key_shuffle, key_offset = jax.random.split(key, 4)
    blocks = OWNERS * SPLITS
    slot_total = blocks * CAP
    heavy = jax.random.randint(key_heavy, (), 0, blocks)
    slot_ids = jnp.arange(slot_total, dtype=jnp.int32)
    slot_device = slot_ids // CAP
    scores = jax.random.randint(key_slots, (blocks, slot_total), 0, 2 ** 12) * slot_total + slot_ids[None, :]
    scores = jnp.where(slot_device[None, :] == heavy, scores - 2 ** 29, scores)
    picked = jnp.argsort(scores, axis=1)[:, :ROWS]
    device_rows = (picked // CAP).astype(jnp.int32)
    shuffle_keys = jax.random.randint(key_shuffle, (blocks, ROWS), 0, 2 ** 16) * ROWS + jnp.arange(ROWS, dtype=jnp.int32)[None, :]
    shuffle = jnp.argsort(shuffle_keys, axis=1)
    device_rows = jnp.take_along_axis(device_rows, shuffle, axis=1)
    onehot = (device_rows[:, :, None] == jnp.arange(blocks, dtype=jnp.int32)[None, None, :]).astype(jnp.int32)
    ranking = jnp.sum((jnp.cumsum(onehot, axis=1) - 1) * onehot, axis=2)
    offsets = jax.random.randint(key_offset, (blocks, blocks), 0, CLUS_DEV)
    offset_rows = jnp.take_along_axis(offsets, device_rows, axis=1)
    chosen = (offset_rows + ranking) % CLUS_DEV
    owner_part = device_rows // SPLITS
    split_part = device_rows % SPLITS
    clusters = owner_part + OWNERS * (split_part + SPLITS * chosen)
    return clusters.reshape(DOCS).astype(jnp.int32)


def draw_cluster_id(key, part):
    return route_draw(key)


def draw_embeddings(key, part):
    clusters = route_draw(key)
    key = jax.random.fold_in(key, 7)
    key_center, key_noise, key_weight, key_scale = jax.random.split(key, 4)
    centers = jax.random.normal(key_center, (CLUSTERS, D), jnp.float32)
    weights = jax.random.uniform(key_weight, (DOCS, 1), jnp.float32, 0.2, 2.0)
    noise = jax.random.normal(key_noise, (DOCS, D), jnp.float32)
    scales = jnp.exp(jax.random.uniform(key_scale, (DOCS, 1), jnp.float32, 0.0, math.log(10.0)))
    values = scales * (weights * centers[clusters] + noise)
    return values.astype(jnp.bfloat16)


def setup_inputs(seed: int = 0) -> dict:
    key_list = jax.random.split(jax.random.key(seed), 4)
    return {
        "embeddings": draw_embeddings(jax.random.fold_in(key_list[3], 71), 0),
        "cluster_id": draw_cluster_id(jax.random.fold_in(key_list[3], 71), 0),
        "doc_order": jax.random.permutation(key_list[2], DOCS).astype(jnp.int32),
    }


def reference(embeddings, cluster_id, doc_order):
    values = embeddings.astype(jnp.float32)
    scaled = values * lax.rsqrt(lax.optimization_barrier(jnp.sum(values * values, axis=1, keepdims=True)) + 1e-06)
    unit_rows = scaled.astype(jnp.bfloat16)
    window = OWNERS * SPLITS
    by_order = jnp.argsort(doc_order, stable=True).astype(jnp.int32)
    by_cluster = jnp.argsort(cluster_id[by_order], stable=True).astype(jnp.int32)
    sorting = by_order[by_cluster]
    sorted_units = jnp.concatenate([jnp.zeros((window, D), jnp.bfloat16), unit_rows[sorting]], axis=0)
    sorted_cluster = jnp.concatenate([jnp.full((window,), -1, jnp.int32), cluster_id[sorting].astype(jnp.int32)], axis=0)
    sorted_order = jnp.concatenate([jnp.zeros((window,), jnp.int32), doc_order[sorting].astype(jnp.int32)], axis=0)
    block_rows = math.gcd(DOCS, 512)

    def one_block(block_index):
        start = (block_index * block_rows).astype(jnp.int32)
        queries = lax.dynamic_slice_in_dim(sorted_units, start + window, block_rows, 0).astype(jnp.float32)
        query_cluster = lax.dynamic_slice_in_dim(sorted_cluster, start + window, block_rows, 0)
        query_order = lax.dynamic_slice_in_dim(sorted_order, start + window, block_rows, 0)
        keys = lax.dynamic_slice_in_dim(sorted_units, start, block_rows + window, 0).astype(jnp.float32)
        key_cluster = lax.dynamic_slice_in_dim(sorted_cluster, start, block_rows + window, 0)
        key_order = lax.dynamic_slice_in_dim(sorted_order, start, block_rows + window, 0)
        scores = jnp.dot(queries, keys.T, preferred_element_type=jnp.float32)
        admitted = (query_cluster[:, None] == key_cluster[None, :]) & (key_order[None, :] < query_order[:, None])
        return lax.optimization_barrier(jnp.max(jnp.where(admitted, scores, -1.0), axis=1))
    highest = lax.map(one_block, jnp.arange(DOCS // block_rows, dtype=jnp.int32)).reshape(DOCS)
    return jnp.zeros((DOCS,), jnp.float32).at[sorting].set(highest)
```

```python
import jax
import jax.numpy as jnp
from jax import lax
from jax.experimental import pallas as pl
from jax.experimental.pallas import tpu as pltpu
from jax.sharding import PartitionSpec as P

MESH = pl.DeviceIdType.MESH
F32 = jnp.float32
BF16 = jnp.bfloat16

NY, NX, NZ, NC = 4, 4, 8, 2
NO, NS = NY * NX, NZ * NC
CAP = 4
ROWS = 512
DIM = 1024
QUART = DIM // 4
SLOTS = NO * NS * CAP
UNIT = NS * CAP
SLAB = 16
BLOCK = NS * SLAB


def iota(shape, dim):
    return lax.broadcasted_iota(jnp.int32, shape, dim)


def dot(a, b, contract):
    return lax.dot_general(a, b, ((contract[:1], contract[1:]), ((), ())), preferred_element_type=F32)


def kernel(
    emb_ref, clu_ref, ord_ref, out_ref,
    unit, onehot, slot, send, recv, keys, meta_out, meta_mid, meta_in, meta_col,
    best_col, best_row, ans_out, ans_mid, ans_in,
    send_sem, recv_sem, ma_s, ma_r, mb_s, mb_r, aa_s, aa_r, ab_s, ab_r, ready,
):
    me_o = lax.axis_index("owner")
    me_s = lax.axis_index("split")
    y, x = me_o // NX, lax.rem(me_o, NX)
    z, c = me_s // NC, lax.rem(me_s, NC)

    def owner_at(k, sign=1):
        dy, dx = k // NX, k % NX
        if sign < 0:
            dy, dx = NY - dy, NX - dx
        return lax.rem(y + dy, NY) * NX + lax.rem(x + dx, NX)

    def split_at(k, sign=1):
        dz, dc = k // NC, k % NC
        if sign < 0:
            dz = NZ - dz
        return lax.rem(z + dz, NZ) * NC + lax.rem(c + dc, NC)

    def remote(src, dst, ssem, rsem, device):
        return pltpu.make_async_remote_copy(
            src_ref=src, dst_ref=dst, send_sem=ssem, recv_sem=rsem,
            device_id=device, device_id_type=MESH,
        )

    barrier = pltpu.get_barrier_semaphore()
    for k in range(1, NS):
        pl.semaphore_signal(barrier, inc=1, device_id=(me_o, split_at(k)), device_id_type=MESH)
    for k in range(1, NO):
        pl.semaphore_signal(barrier, inc=1, device_id=(owner_at(k), me_s), device_id_type=MESH)

    clu = clu_ref[...]
    orders = ord_ref[...]
    to_o = clu & (NO - 1)
    to_s = (clu >> 4) & (NS - 1)
    rel_y = ((to_o >> 2) - y) & (NY - 1)
    rel_x = ((to_o & (NX - 1)) - x) & (NX - 1)
    rel_z = ((to_s >> 1) - z) & (NZ - 1)
    rel_c = ((to_s & 1) - c) & 1
    k_o = rel_y * NX + rel_x
    k_s = rel_z * NC + rel_c
    goal = k_o * NS + k_s
    hot = (goal == iota((NO * NS, ROWS), 0)).astype(F32)
    onehot[...] = hot.astype(BF16)
    before = (iota((ROWS, ROWS), 0) < iota((ROWS, ROWS), 1)).astype(F32).astype(BF16)
    count = dot(onehot[...], before, (1, 0))
    rank = jnp.sum(hot * count, axis=0, keepdims=True).astype(jnp.int32)
    slot[...] = k_o * UNIT + rank * NS + k_s

    line = iota((8, ROWS), 0)
    code = clu + 1
    parts = jnp.where(
        line == 0, orders >> 12,
        jnp.where(line == 1, (orders >> 6) & 63,
                  jnp.where(line == 2, orders & 63,
                            jnp.where(line == 3, code >> 6,
                                      jnp.where(line == 4, code & 63, 0)))),
    ).astype(F32).astype(BF16)
    by_split = k_s * UNIT + k_o * CAP + rank
    pick = (by_split == iota((SLOTS, ROWS), 0)).astype(F32).astype(BF16)
    got = dot(parts, pick, (1, 1))
    slot_order = got[0:1] * 4096.0 + got[1:2] * 64.0 + got[2:3]
    slot_cluster = got[3:4] * 64.0 + got[4:5] - 1.0
    low = iota((1, 128), 1) < 64
    for p in range(NS // 2):
        a = slot_order[:, p * 128 : (p + 1) * 128]
        b = slot_cluster[:, p * 128 : (p + 1) * 128]
        meta_out[2 * p] = jnp.where(low, a, pltpu.roll(b, 64, 1))
        meta_out[2 * p + 1] = jnp.where(low, pltpu.roll(a, 64, 1), b)

    values = emb_ref[...].astype(F32)
    scale = lax.rsqrt(jnp.sum(values * values, axis=1, keepdims=True) + 1e-06)
    unit[...] = (values * scale).astype(BF16)

    pl.semaphore_wait(barrier, NS - 1 + NO - 1)
    for k in range(1, NO):
        pl.semaphore_signal(ready, inc=1, device_id=(owner_at(k), me_s), device_id_type=MESH)
    for k in range(1, NS):
        remote(meta_out.at[k], meta_mid.at[k], ma_s, ma_r, (me_o, split_at(k))).start()
    meta_mid[0] = meta_out[0]
    pl.semaphore_wait(ready, NO - 1)

    row, col = iota((BLOCK, BLOCK), 0), iota((BLOCK, BLOCK), 1)
    weave = (
        col == ((row >> 2) & 3) * UNIT + (row & 3) * NS + (row >> 4)
    ).astype(F32).astype(BF16)
    unweave = (
        row == ((col >> 2) & 3) * UNIT + (col & 3) * NS + (col >> 4)
    ).astype(F32).astype(BF16)

    for b in range(NO):
        choose = (slot[...] == b * UNIT + iota((UNIT, ROWS), 0)).astype(F32).astype(BF16)
        rows = dot(choose, unit[...], (1, 0)).astype(BF16)
        quarters = jnp.concatenate([rows[:, q * QUART : (q + 1) * QUART] for q in range(4)], axis=0)
        send[b * BLOCK : (b + 1) * BLOCK] = dot(weave, quarters, (1, 0)).astype(BF16)
        for k in range(NS):
            part = pl.ds(b * BLOCK + k * SLAB, SLAB)
            if b == 0 and k == 0:
                recv[part] = send[part]
                continue
            remote(
                send.at[part], recv.at[part], send_sem.at[b], recv_sem.at[b],
                (owner_at(b), split_at(k)),
            ).start()

    some = remote(meta_out.at[pl.ds(1, NS - 1)], meta_mid.at[pl.ds(1, NS - 1)], ma_s, ma_r, (me_o, split_at(1)))
    some.wait_recv()
    for k in range(1, NO):
        remote(meta_mid, meta_in.at[k], mb_s, mb_r, (owner_at(k), me_s)).start()
    meta_in[0] = meta_mid[...]
    some.wait_send()
    many = remote(meta_in.at[pl.ds(1, NO - 1)], meta_in.at[pl.ds(1, NO - 1)], mb_s, mb_r, (owner_at(1), me_s))
    many.wait_recv()
    for b in range(NO):
        lines = meta_in[b].reshape(NS, 128)
        for r in range(CAP):
            at = b * UNIT + r * NS
            lane = b * CAP + r
            meta_col[at : at + NS] = pltpu.roll(lines, 128 - lane, 1) if lane else lines
    many.wait_send()
    turned = meta_col[...].T
    row_order, row_cluster = turned[0:1], turned[64:65]

    best_row[...] = jnp.full((1, SLOTS), -1.0, F32)
    step = 2
    for g in range(0, NO, step):
        for b in range(g, g + step):
            first = SLAB if b == 0 else 0
            span = pl.ds(b * BLOCK + first, BLOCK - first)
            remote(
                send.at[span], recv.at[span], send_sem.at[b], recv_sem.at[b], (me_o, split_at(1))
            ).wait_recv()
            woven = dot(unweave, recv[b * BLOCK : (b + 1) * BLOCK], (1, 0)).astype(BF16)
            for q in range(4):
                keys[b * UNIT : (b + 1) * UNIT, q * QUART : (q + 1) * QUART] = woven[
                    q * UNIT : (q + 1) * UNIT
                ]
        lo, hi = g * UNIT, (g + step) * UNIT
        score = dot(keys[lo:hi], keys[0:hi], (1, 1))
        new_order, new_cluster = meta_col[lo:hi, 0:1], meta_col[lo:hi, 64:65]
        old_order, old_cluster = row_order[:, :hi], row_cluster[:, :hi]
        score = jnp.where(new_cluster == old_cluster, score, -1.0)
        best = jnp.max(jnp.where(old_order < new_order, score, -1.0), axis=1, keepdims=True)
        best_col[lo:hi] = jnp.broadcast_to(best, (hi - lo, 128))
        best = jnp.max(jnp.where(new_order < old_order, score, -1.0), axis=0, keepdims=True)
        best_row[:, :hi] = jnp.maximum(best_row[:, :hi], best)

    final = jnp.maximum(best_col[...], jnp.broadcast_to(best_row[...], (128, SLOTS)).T)
    lanes = iota((NS, 128), 1)
    answer = jnp.zeros((NS, 128), F32)
    for u in range(UNIT):
        answer = jnp.where(lanes == u, final[u * NS : (u + 1) * NS], answer)
    ans_out[...] = answer.reshape(NS, 1, 128)
    for k in range(1, NS):
        remote(ans_out.at[k], ans_mid.at[k], aa_s, aa_r, (me_o, split_at(k, -1))).start()
    ans_mid[0] = ans_out[0]
    some = remote(ans_out.at[pl.ds(1, NS - 1)], ans_mid.at[pl.ds(1, NS - 1)], aa_s, aa_r, (me_o, split_at(1)))
    some.wait_recv()
    for k in range(1, NO):
        remote(ans_mid, ans_in.at[k], ab_s, ab_r, (owner_at(k, -1), me_s)).start()
    ans_in[0] = ans_mid[...]
    some.wait_send()
    many = remote(ans_in.at[pl.ds(1, NO - 1)], ans_in.at[pl.ds(1, NO - 1)], ab_s, ab_r, (owner_at(1), me_s))
    many.wait_recv()

    table = ans_in[...].reshape(NO * NS, 128).T
    high = table.astype(BF16)
    rest = table - high.astype(F32)
    mid = rest.astype(BF16)
    tiny = (rest - mid.astype(F32)).astype(BF16)
    mine = dot(high, onehot[...], (1, 0)) + dot(mid, onehot[...], (1, 0)) + dot(tiny, onehot[...], (1, 0))
    place = k_o * CAP + rank
    out_ref[...] = jnp.sum(jnp.where(iota((128, ROWS), 0) == place, mine, 0.0), axis=0, keepdims=True)

    many.wait_send()
    for b in range(NO):
        first = SLAB if b == 0 else 0
        span = pl.ds(b * BLOCK + first, BLOCK - first)
        remote(
            send.at[span], recv.at[span], send_sem.at[b], recv_sem.at[b], (me_o, split_at(1))
        ).wait_send()


def local(embeddings, cluster_id, doc_order):
    vmem = pl.BlockSpec(memory_space=pltpu.VMEM)
    dma = pltpu.SemaphoreType.DMA
    out = pl.pallas_call(
        kernel,
        name="dedup",
        out_shape=jax.ShapeDtypeStruct((1, ROWS), F32),
        in_specs=[vmem] * 3,
        out_specs=vmem,
        scratch_shapes=[
            pltpu.VMEM((ROWS, DIM), BF16),
            pltpu.VMEM((NO * NS, ROWS), BF16),
            pltpu.VMEM((1, ROWS), jnp.int32),
            pltpu.VMEM((NO * BLOCK, QUART), BF16),
            pltpu.VMEM((NO * BLOCK, QUART), BF16),
            pltpu.VMEM((SLOTS, DIM), BF16),
            pltpu.VMEM((NS, 1, 128), F32),
            pltpu.VMEM((NS, 1, 128), F32),
            pltpu.VMEM((NO, NS, 1, 128), F32),
            pltpu.VMEM((SLOTS, 128), F32),
            pltpu.VMEM((SLOTS, 128), F32),
            pltpu.VMEM((1, SLOTS), F32),
            pltpu.VMEM((NS, 1, 128), F32),
            pltpu.VMEM((NS, 1, 128), F32),
            pltpu.VMEM((NO, NS, 1, 128), F32),
            dma((NO,)), dma((NO,)),
            dma, dma, dma, dma, dma, dma, dma, dma,
            pltpu.SemaphoreType.REGULAR,
        ],
        compiler_params=pltpu.CompilerParams(
            collective_id=0, has_side_effects=True, vmem_limit_bytes=48 << 20
        ),
        cost_estimate=pl.CostEstimate(
            flops=8 << 30, bytes_accessed=4 << 20, transcendentals=ROWS
        ),
    )(embeddings, cluster_id.reshape(1, ROWS), doc_order.reshape(1, ROWS))
    return out.reshape(ROWS)


def solution(mesh):
    in_specs = (P(("owner", "split"), None), P(("owner", "split")), P(("owner", "split")))
    out_specs = P(("owner", "split"))
    return jax.shard_map(local, mesh=mesh, in_specs=in_specs, out_specs=out_specs, check_vma=False)
```

```python
import jax
import jax.numpy as jnp
from jax import lax
from jax.experimental import pallas as pl
from jax.experimental.pallas import tpu as pltpu
from jax.sharding import PartitionSpec as P

MESH = pl.DeviceIdType.MESH
F32 = jnp.float32
BF16 = jnp.bfloat16

NY, NX, NZ, NC = 4, 4, 8, 2
NO, NS = NY * NX, NZ * NC
CAP = 4
ROWS = 512
DIM = 1024
QUART = DIM // 4
SLOTS = NO * NS * CAP
UNIT = NS * CAP
SLAB = 16
BLOCK = NS * SLAB
CHIPS = NO * NZ


def distance(k):
    dy, dx = divmod(k, NX)
    return min(dy, NY - dy) + min(dx, NX - dx)


STEPS = [0] + sorted(range(1, NO), key=lambda k: -distance(k))
SPLITS = sorted(range(NS), key=lambda k: -min(k % NZ, NZ - k % NZ))


def iota(shape, dim):
    return lax.broadcasted_iota(jnp.int32, shape, dim)


def dot(a, b, contract):
    return lax.dot_general(a, b, ((contract[:1], contract[1:]), ((), ())), preferred_element_type=F32)


def ones_where(mask):
    return mask.astype(F32).astype(BF16)


def kernel(
    emb_hbm, clu_hbm, ord_hbm, out_ref,
    emb, clu_v, ord_v, onehot, slot, send, recv, keys, meta_out, meta_mid, meta_in, meta_col,
    best_col, best_row, swap_out, swap_in, ans_out, ans_in,
    in_sem, send_sem, recv_sem, ma_s, ma_r, mb_s, mb_r, sw_s, sw_r, an_s, an_r, ready,
):
    me_o = lax.axis_index("owner")
    me_s = lax.axis_index("split")
    y, x = me_o // NX, lax.rem(me_o, NX)
    z, c = me_s // NC, lax.rem(me_s, NC)

    def owner_at(k, sign=1):
        dy, dx = k // NX, k % NX
        if sign < 0:
            dy, dx = NY - dy, NX - dx
        return lax.rem(y + dy, NY) * NX + lax.rem(x + dx, NX)

    def split_at(k, sign=1):
        dc, dz = k // NZ, k % NZ
        if sign < 0:
            dz = NZ - dz
        return lax.rem(z + dz, NZ) * NC + lax.rem(c + dc, NC)

    def remote(src, dst, ssem, rsem, device):
        return pltpu.make_async_remote_copy(
            src_ref=src, dst_ref=dst, send_sem=ssem, recv_sem=rsem,
            device_id=device, device_id_type=MESH,
        )

    clu_in = pltpu.make_async_copy(clu_hbm, clu_v, in_sem.at[0])
    emb_in = pltpu.make_async_copy(emb_hbm, emb, in_sem.at[1])
    ord_in = pltpu.make_async_copy(ord_hbm, ord_v, in_sem.at[2])
    clu_in.start()
    emb_in.start()
    ord_in.start()

    barrier = pltpu.get_barrier_semaphore()
    for k in SPLITS:
        if k:
            pl.semaphore_signal(barrier, inc=1, device_id=(me_o, split_at(k)), device_id_type=MESH)
    for k in STEPS[1:]:
        pl.semaphore_signal(barrier, inc=1, device_id=(owner_at(k), me_s), device_id_type=MESH)

    before = ones_where(iota((ROWS, ROWS), 0) < iota((ROWS, ROWS), 1))
    row, col = iota((BLOCK, BLOCK), 0), iota((BLOCK, BLOCK), 1)
    weave = ones_where(col == ((row >> 2) & 3) * UNIT + (row & 3) * NS + (row >> 4))
    unweave = ones_where(row == ((col >> 2) & 3) * UNIT + (col & 3) * NS + (col >> 4))

    clu_in.wait()
    clu = clu_v[...]
    to_o = clu & (NO - 1)
    to_s = (clu >> 4) & (NS - 1)
    rel_y = ((to_o >> 2) - y) & (NY - 1)
    rel_x = ((to_o & (NX - 1)) - x) & (NX - 1)
    rel_z = ((to_s >> 1) - z) & (NZ - 1)
    rel_c = ((to_s & 1) - c) & 1
    k_o = rel_y * NX + rel_x
    k_s = rel_c * NZ + rel_z
    hot = (k_o * NS + k_s == iota((NO * NS, ROWS), 0)).astype(F32)
    count = dot(hot.astype(BF16), before, (1, 0))
    rank = jnp.sum(hot * count, axis=0, keepdims=True).astype(jnp.int32)
    slot[...] = k_o * UNIT + rank * NS + k_s

    def fill(b):
        choose = ones_where(slot[...] == b * UNIT + iota((UNIT, ROWS), 0))
        rows = dot(choose, emb[...], (1, 0))
        scale = lax.rsqrt(jnp.sum(rows * rows, axis=1, keepdims=True) + 1e-06)
        rows = (rows * scale).astype(BF16)
        quarters = jnp.concatenate([rows[:, q * QUART : (q + 1) * QUART] for q in range(4)], axis=0)
        send[b * BLOCK : (b + 1) * BLOCK] = dot(weave, quarters, (1, 0)).astype(BF16)

    def ship(b):
        for k in SPLITS:
            part = pl.ds(b * BLOCK + k * SLAB, SLAB)
            if b == 0 and k == 0:
                recv[part] = send[part]
                continue
            remote(
                send.at[part], recv.at[part], send_sem.at[b], recv_sem.at[b],
                (owner_at(b), split_at(k)),
            ).start()

    emb_in.wait()
    fill(0)
    pl.semaphore_wait(barrier, NS - 1 + NO - 1)
    for k in STEPS[1:]:
        pl.semaphore_signal(ready.at[k], inc=1, device_id=(owner_at(k, -1), me_s), device_id_type=MESH)
    ship(0)

    onehot[...] = ones_where(k_o * NZ + rel_z == iota((CHIPS, ROWS), 0))
    ord_in.wait()
    orders = ord_v[...]
    line = iota((8, ROWS), 0)
    code = clu + 1
    parts = jnp.where(
        line == 0, orders >> 12,
        jnp.where(line == 1, (orders >> 6) & 63,
                  jnp.where(line == 2, orders & 63,
                            jnp.where(line == 3, code >> 6,
                                      jnp.where(line == 4, code & 63, 0)))),
    ).astype(F32).astype(BF16)
    by_split = k_s * UNIT + k_o * CAP + rank
    pick = ones_where(by_split == iota((SLOTS, ROWS), 0))
    got = dot(parts, pick, (1, 1))
    slot_order = got[0:1] * 4096.0 + got[1:2] * 64.0 + got[2:3]
    slot_cluster = got[3:4] * 64.0 + got[4:5] - 1.0
    low = iota((1, 128), 1) < 64
    for p in range(NS // 2):
        a = slot_order[:, p * 128 : (p + 1) * 128]
        b = slot_cluster[:, p * 128 : (p + 1) * 128]
        meta_out[2 * p] = jnp.where(low, a, pltpu.roll(b, 64, 1))
        meta_out[2 * p + 1] = jnp.where(low, pltpu.roll(a, 64, 1), b)
    for k in SPLITS:
        if k:
            remote(meta_out.at[k], meta_mid.at[k], ma_s, ma_r, (me_o, split_at(k))).start()
    meta_mid[0] = meta_out[0]

    for b in STEPS[1:]:
        fill(b)
        pl.semaphore_wait(ready.at[b], 1)
        ship(b)

    some = remote(meta_out.at[pl.ds(1, NS - 1)], meta_mid.at[pl.ds(1, NS - 1)], ma_s, ma_r, (me_o, split_at(1)))
    some.wait_recv()
    for k in STEPS[1:]:
        remote(meta_mid, meta_in.at[k], mb_s, mb_r, (owner_at(k), me_s)).start()
    meta_in[0] = meta_mid[...]
    some.wait_send()
    many = remote(meta_in.at[pl.ds(1, NO - 1)], meta_in.at[pl.ds(1, NO - 1)], mb_s, mb_r, (owner_at(1), me_s))
    many.wait_recv()
    for i, b in enumerate(STEPS):
        lines = meta_in[b].reshape(NS, 128)
        for r in range(CAP):
            at = i * UNIT + r * NS
            lane = b * CAP + r
            meta_col[at : at + NS] = pltpu.roll(lines, 128 - lane, 1) if lane else lines
    many.wait_send()
    turned = meta_col[...].T
    row_order, row_cluster = turned[0:1], turned[64:65]

    best_row[...] = jnp.full((1, SLOTS), -1.0, F32)
    step = 2
    for g in range(0, NO, step):
        for i in range(g, g + step):
            b = STEPS[i]
            first = SLAB if b == 0 else 0
            span = pl.ds(b * BLOCK + first, BLOCK - first)
            remote(
                send.at[span], recv.at[span], send_sem.at[b], recv_sem.at[b], (me_o, split_at(1))
            ).wait_recv()
            woven = dot(unweave, recv[b * BLOCK : (b + 1) * BLOCK], (1, 0)).astype(BF16)
            for q in range(4):
                keys[i * UNIT : (i + 1) * UNIT, q * QUART : (q + 1) * QUART] = woven[
                    q * UNIT : (q + 1) * UNIT
                ]
        lo, hi = g * UNIT, (g + step) * UNIT
        score = dot(keys[lo:hi], keys[0:hi], (1, 1))
        new_order, new_cluster = meta_col[lo:hi, 0:1], meta_col[lo:hi, 64:65]
        old_order, old_cluster = row_order[:, :hi], row_cluster[:, :hi]
        score = jnp.where(new_cluster == old_cluster, score, -1.0)
        best = jnp.max(jnp.where(old_order < new_order, score, -1.0), axis=1, keepdims=True)
        best_col[lo:hi] = jnp.broadcast_to(best, (hi - lo, 128))
        best = jnp.max(jnp.where(new_order < old_order, score, -1.0), axis=0, keepdims=True)
        best_row[:, :hi] = jnp.maximum(best_row[:, :hi], best)

    final = jnp.maximum(best_col[...], jnp.broadcast_to(best_row[...], (128, SLOTS)).T)
    lanes = iota((NZ, 128), 1)
    for i, b in enumerate(STEPS):
        stay = jnp.zeros((NZ, 128), F32)
        leave = jnp.zeros((NZ, 128), F32)
        for r in range(CAP):
            at = i * UNIT + r * NS
            stay = jnp.where(lanes == r, final[at : at + NZ], stay)
            leave = jnp.where(lanes == CAP + r, final[at + NZ : at + NS], leave)
        swap_out[b * NZ : (b + 1) * NZ] = leave
        best_col[b * NZ : (b + 1) * NZ] = stay
    swap = remote(swap_out, swap_in, sw_s, sw_r, (me_o, split_at(NZ)))
    swap.start()
    swap.wait_recv()
    both = best_col[0:CHIPS] + swap_in[...]
    ans_out[...] = both.reshape(CHIPS, 1, 128)
    ways = sorted(range(1, CHIPS), key=lambda k: -distance(k // NZ) - min(k % NZ, NZ - k % NZ))
    for k in ways:
        remote(
            ans_out.at[k], ans_in.at[k], an_s, an_r, (owner_at(k // NZ, -1), split_at(k % NZ, -1))
        ).start()
    ans_in[0] = ans_out[0]
    swap.wait_send()
    for b in range(NO):
        first = SLAB if b == 0 else 0
        span = pl.ds(b * BLOCK + first, BLOCK - first)
        remote(
            send.at[span], recv.at[span], send_sem.at[b], recv_sem.at[b], (me_o, split_at(1))
        ).wait_send()
    most = pl.ds(1, CHIPS - 1)
    answers = remote(ans_out.at[most], ans_in.at[most], an_s, an_r, (me_o, split_at(1)))
    answers.wait_recv()

    table = ans_in[...].reshape(CHIPS, 128).T[0:8]
    high = table.astype(BF16)
    rest = table - high.astype(F32)
    mid = rest.astype(BF16)
    tiny = (rest - mid.astype(F32)).astype(BF16)
    mine = dot(high, onehot[...], (1, 0)) + dot(mid, onehot[...], (1, 0)) + dot(tiny, onehot[...], (1, 0))
    out_ref[...] = jnp.sum(jnp.where(line == rel_c * CAP + rank, mine, 0.0), axis=0, keepdims=True)
    answers.wait_send()


def local(embeddings, cluster_id, doc_order):
    hbm = pl.BlockSpec(memory_space=pltpu.HBM)
    dma = pltpu.SemaphoreType.DMA
    out = pl.pallas_call(
        kernel,
        name="dedup",
        out_shape=jax.ShapeDtypeStruct((1, ROWS), F32),
        in_specs=[hbm] * 3,
        out_specs=pl.BlockSpec(memory_space=pltpu.VMEM),
        scratch_shapes=[
            pltpu.VMEM((ROWS, DIM), BF16),
            pltpu.VMEM((1, ROWS), jnp.int32),
            pltpu.VMEM((1, ROWS), jnp.int32),
            pltpu.VMEM((CHIPS, ROWS), BF16),
            pltpu.VMEM((1, ROWS), jnp.int32),
            pltpu.VMEM((NO * BLOCK, QUART), BF16),
            pltpu.VMEM((NO * BLOCK, QUART), BF16),
            pltpu.VMEM((SLOTS, DIM), BF16),
            pltpu.VMEM((NS, 1, 128), F32),
            pltpu.VMEM((NS, 1, 128), F32),
            pltpu.VMEM((NO, NS, 1, 128), F32),
            pltpu.VMEM((SLOTS, 128), F32),
            pltpu.VMEM((SLOTS, 128), F32),
            pltpu.VMEM((1, SLOTS), F32),
            pltpu.VMEM((CHIPS, 128), F32),
            pltpu.VMEM((CHIPS, 128), F32),
            pltpu.VMEM((CHIPS, 1, 128), F32),
            pltpu.VMEM((CHIPS, 1, 128), F32),
            dma((3,)), dma((NO,)), dma((NO,)),
            dma, dma, dma, dma, dma, dma, dma, dma,
            pltpu.SemaphoreType.REGULAR((NO,)),
        ],
        compiler_params=pltpu.CompilerParams(
            collective_id=0, has_side_effects=True, vmem_limit_bytes=56 << 20
        ),
        cost_estimate=pl.CostEstimate(
            flops=8 << 30, bytes_accessed=4 << 20, transcendentals=SLOTS
        ),
    )(embeddings, cluster_id.reshape(1, ROWS), doc_order.reshape(1, ROWS))
    return out.reshape(ROWS)


def solution(mesh):
    in_specs = (P(("owner", "split"), None), P(("owner", "split")), P(("owner", "split")))
    out_specs = P(("owner", "split"))
    return jax.shard_map(local, mesh=mesh, in_specs=in_specs, out_specs=out_specs, check_vma=False)
```

```python
import jax
import jax.numpy as jnp
from jax import lax
from jax.experimental import pallas as pl
from jax.experimental.pallas import tpu as pltpu
from jax.sharding import PartitionSpec as P

MESH = pl.DeviceIdType.MESH
F32 = jnp.float32
BF16 = jnp.bfloat16

NY, NX, NZ, NC = 4, 4, 8, 2
NO, NS = NY * NX, NZ * NC
CAP = 4
ROWS = 512
DIM = 1024
QUART = DIM // 4
SLOTS = NO * NS * CAP
UNIT = NS * CAP
SLAB = 16
BLOCK = NS * SLAB
CHIPS = NO * NZ

NEAR = 2
PAIR = NS * NEAR
LEAF = 16
EIGHTH = DIM // 8
POOL = 32
POOLED = NZ * POOL
TAIL = NZ * (CAP - NEAR)
BLOCKS = NO * NC
FIRST = 8
EARLY = 12
POOL_AT = EARLY * PAIR
FLAG = 2.0**18
REDO = 4.0


def distance(k):
    dy, dx = divmod(k, NX)
    return min(dy, NY - dy) + min(dx, NX - dx)


STEPS = [0] + sorted(range(1, NO), key=lambda k: -distance(k))
SPLITS = sorted(range(NS), key=lambda k: -min(k % NZ, NZ - k % NZ))


def iota(shape, dim):
    return lax.broadcasted_iota(jnp.int32, shape, dim)


def dot(a, b, contract):
    return lax.dot_general(a, b, ((contract[:1], contract[1:]), ((), ())), preferred_element_type=F32)


def ones_where(mask):
    return mask.astype(F32).astype(BF16)


def full_kernel(
    emb_hbm, clu_hbm, ord_hbm, out_ref,
    emb, clu_v, ord_v, onehot, slot, send, recv, keys, meta_out, meta_mid, meta_in, meta_col,
    best_col, best_row, swap_out, swap_in, ans_out, ans_in,
    in_sem, send_sem, recv_sem, ma_s, ma_r, mb_s, mb_r, sw_s, sw_r, an_s, an_r, ready,
):
    me_o = lax.axis_index("owner")
    me_s = lax.axis_index("split")
    y, x = me_o // NX, lax.rem(me_o, NX)
    z, c = me_s // NC, lax.rem(me_s, NC)

    def owner_at(k, sign=1):
        dy, dx = k // NX, k % NX
        if sign < 0:
            dy, dx = NY - dy, NX - dx
        return lax.rem(y + dy, NY) * NX + lax.rem(x + dx, NX)

    def split_at(k, sign=1):
        dc, dz = k // NZ, k % NZ
        if sign < 0:
            dz = NZ - dz
        return lax.rem(z + dz, NZ) * NC + lax.rem(c + dc, NC)

    def remote(src, dst, ssem, rsem, device):
        return pltpu.make_async_remote_copy(
            src_ref=src, dst_ref=dst, send_sem=ssem, recv_sem=rsem,
            device_id=device, device_id_type=MESH,
        )

    clu_in = pltpu.make_async_copy(clu_hbm, clu_v, in_sem.at[0])
    emb_in = pltpu.make_async_copy(emb_hbm, emb, in_sem.at[1])
    ord_in = pltpu.make_async_copy(ord_hbm, ord_v, in_sem.at[2])
    clu_in.start()
    emb_in.start()
    ord_in.start()

    barrier = pltpu.get_barrier_semaphore()
    for k in SPLITS:
        if k:
            pl.semaphore_signal(barrier, inc=1, device_id=(me_o, split_at(k)), device_id_type=MESH)
    for k in STEPS[1:]:
        pl.semaphore_signal(barrier, inc=1, device_id=(owner_at(k), me_s), device_id_type=MESH)

    before = ones_where(iota((ROWS, ROWS), 0) < iota((ROWS, ROWS), 1))
    row, col = iota((BLOCK, BLOCK), 0), iota((BLOCK, BLOCK), 1)
    weave = ones_where(col == ((row >> 2) & 3) * UNIT + (row & 3) * NS + (row >> 4))
    unweave = ones_where(row == ((col >> 2) & 3) * UNIT + (col & 3) * NS + (col >> 4))

    clu_in.wait()
    clu = clu_v[...]
    to_o = clu & (NO - 1)
    to_s = (clu >> 4) & (NS - 1)
    rel_y = ((to_o >> 2) - y) & (NY - 1)
    rel_x = ((to_o & (NX - 1)) - x) & (NX - 1)
    rel_z = ((to_s >> 1) - z) & (NZ - 1)
    rel_c = ((to_s & 1) - c) & 1
    k_o = rel_y * NX + rel_x
    k_s = rel_c * NZ + rel_z
    hot = (k_o * NS + k_s == iota((NO * NS, ROWS), 0)).astype(F32)
    count = dot(hot.astype(BF16), before, (1, 0))
    rank = jnp.sum(hot * count, axis=0, keepdims=True).astype(jnp.int32)
    slot[...] = k_o * UNIT + rank * NS + k_s

    def fill(b):
        choose = ones_where(slot[...] == b * UNIT + iota((UNIT, ROWS), 0))
        rows = dot(choose, emb[...], (1, 0))
        scale = lax.rsqrt(jnp.sum(rows * rows, axis=1, keepdims=True) + 1e-06)
        rows = (rows * scale).astype(BF16)
        quarters = jnp.concatenate([rows[:, q * QUART : (q + 1) * QUART] for q in range(4)], axis=0)
        send[b * BLOCK : (b + 1) * BLOCK] = dot(weave, quarters, (1, 0)).astype(BF16)

    def ship(b):
        for k in SPLITS:
            part = pl.ds(b * BLOCK + k * SLAB, SLAB)
            if b == 0 and k == 0:
                recv[part] = send[part]
                continue
            remote(
                send.at[part], recv.at[part], send_sem.at[b], recv_sem.at[b],
                (owner_at(b), split_at(k)),
            ).start()

    emb_in.wait()
    fill(0)
    pl.semaphore_wait(barrier, NS - 1 + NO - 1)
    for k in STEPS[1:]:
        pl.semaphore_signal(ready.at[k], inc=1, device_id=(owner_at(k, -1), me_s), device_id_type=MESH)
    ship(0)

    onehot[...] = ones_where(k_o * NZ + rel_z == iota((CHIPS, ROWS), 0))
    ord_in.wait()
    orders = ord_v[...]
    line = iota((8, ROWS), 0)
    code = clu + 1
    parts = jnp.where(
        line == 0, orders >> 12,
        jnp.where(line == 1, (orders >> 6) & 63,
                  jnp.where(line == 2, orders & 63,
                            jnp.where(line == 3, code >> 6,
                                      jnp.where(line == 4, code & 63, 0)))),
    ).astype(F32).astype(BF16)
    by_split = k_s * UNIT + k_o * CAP + rank
    pick = ones_where(by_split == iota((SLOTS, ROWS), 0))
    got = dot(parts, pick, (1, 1))
    slot_order = got[0:1] * 4096.0 + got[1:2] * 64.0 + got[2:3]
    slot_cluster = got[3:4] * 64.0 + got[4:5] - 1.0
    low = iota((1, 128), 1) < 64
    for p in range(NS // 2):
        a = slot_order[:, p * 128 : (p + 1) * 128]
        b = slot_cluster[:, p * 128 : (p + 1) * 128]
        meta_out[2 * p] = jnp.where(low, a, pltpu.roll(b, 64, 1))
        meta_out[2 * p + 1] = jnp.where(low, pltpu.roll(a, 64, 1), b)
    for k in SPLITS:
        if k:
            remote(meta_out.at[k], meta_mid.at[k], ma_s, ma_r, (me_o, split_at(k))).start()
    meta_mid[0] = meta_out[0]

    for b in STEPS[1:]:
        fill(b)
        pl.semaphore_wait(ready.at[b], 1)
        ship(b)

    some = remote(meta_out.at[pl.ds(1, NS - 1)], meta_mid.at[pl.ds(1, NS - 1)], ma_s, ma_r, (me_o, split_at(1)))
    some.wait_recv()
    for k in STEPS[1:]:
        remote(meta_mid, meta_in.at[k], mb_s, mb_r, (owner_at(k), me_s)).start()
    meta_in[0] = meta_mid[...]
    some.wait_send()
    many = remote(meta_in.at[pl.ds(1, NO - 1)], meta_in.at[pl.ds(1, NO - 1)], mb_s, mb_r, (owner_at(1), me_s))
    many.wait_recv()
    for i, b in enumerate(STEPS):
        lines = meta_in[b].reshape(NS, 128)
        for r in range(CAP):
            at = i * UNIT + r * NS
            lane = b * CAP + r
            meta_col[at : at + NS] = pltpu.roll(lines, 128 - lane, 1) if lane else lines
    many.wait_send()
    turned = meta_col[...].T
    row_order, row_cluster = turned[0:1], turned[64:65]

    best_row[...] = jnp.full((1, SLOTS), -1.0, F32)
    step = 2
    for g in range(0, NO, step):
        for i in range(g, g + step):
            b = STEPS[i]
            first = SLAB if b == 0 else 0
            span = pl.ds(b * BLOCK + first, BLOCK - first)
            remote(
                send.at[span], recv.at[span], send_sem.at[b], recv_sem.at[b], (me_o, split_at(1))
            ).wait_recv()
            woven = dot(unweave, recv[b * BLOCK : (b + 1) * BLOCK], (1, 0)).astype(BF16)
            for q in range(4):
                keys[i * UNIT : (i + 1) * UNIT, q * QUART : (q + 1) * QUART] = woven[
                    q * UNIT : (q + 1) * UNIT
                ]
        lo, hi = g * UNIT, (g + step) * UNIT
        score = dot(keys[lo:hi], keys[0:hi], (1, 1))
        new_order, new_cluster = meta_col[lo:hi, 0:1], meta_col[lo:hi, 64:65]
        old_order, old_cluster = row_order[:, :hi], row_cluster[:, :hi]
        score = jnp.where(new_cluster == old_cluster, score, -1.0)
        best = jnp.max(jnp.where(old_order < new_order, score, -1.0), axis=1, keepdims=True)
        best_col[lo:hi] = jnp.broadcast_to(best, (hi - lo, 128))
        best = jnp.max(jnp.where(new_order < old_order, score, -1.0), axis=0, keepdims=True)
        best_row[:, :hi] = jnp.maximum(best_row[:, :hi], best)

    final = jnp.maximum(best_col[...], jnp.broadcast_to(best_row[...], (128, SLOTS)).T)
    lanes = iota((NZ, 128), 1)
    for i, b in enumerate(STEPS):
        stay = jnp.zeros((NZ, 128), F32)
        leave = jnp.zeros((NZ, 128), F32)
        for r in range(CAP):
            at = i * UNIT + r * NS
            stay = jnp.where(lanes == r, final[at : at + NZ], stay)
            leave = jnp.where(lanes == CAP + r, final[at + NZ : at + NS], leave)
        swap_out[b * NZ : (b + 1) * NZ] = leave
        best_col[b * NZ : (b + 1) * NZ] = stay
    swap = remote(swap_out, swap_in, sw_s, sw_r, (me_o, split_at(NZ)))
    swap.start()
    swap.wait_recv()
    both = best_col[0:CHIPS] + swap_in[...]
    ans_out[...] = both.reshape(CHIPS, 1, 128)
    ways = sorted(range(1, CHIPS), key=lambda k: -distance(k // NZ) - min(k % NZ, NZ - k % NZ))
    for k in ways:
        remote(
            ans_out.at[k], ans_in.at[k], an_s, an_r, (owner_at(k // NZ, -1), split_at(k % NZ, -1))
        ).start()
    ans_in[0] = ans_out[0]
    swap.wait_send()
    for b in range(NO):
        first = SLAB if b == 0 else 0
        span = pl.ds(b * BLOCK + first, BLOCK - first)
        remote(
            send.at[span], recv.at[span], send_sem.at[b], recv_sem.at[b], (me_o, split_at(1))
        ).wait_send()
    most = pl.ds(1, CHIPS - 1)
    answers = remote(ans_out.at[most], ans_in.at[most], an_s, an_r, (me_o, split_at(1)))
    answers.wait_recv()

    table = ans_in[...].reshape(CHIPS, 128).T[0:8]
    high = table.astype(BF16)
    rest = table - high.astype(F32)
    mid = rest.astype(BF16)
    tiny = (rest - mid.astype(F32)).astype(BF16)
    mine = dot(high, onehot[...], (1, 0)) + dot(mid, onehot[...], (1, 0)) + dot(tiny, onehot[...], (1, 0))
    out_ref[...] = jnp.sum(jnp.where(line == rel_c * CAP + rank, mine, 0.0), axis=0, keepdims=True)
    answers.wait_send()


def pooled_kernel(
    emb_hbm, clu_hbm, ord_hbm, out_ref,
    emb, clu_v, ord_v, onehot, slot, send, recv, keys, meta_out, meta_mid, meta_in, meta_col,
    best_col, best_row, swap_out, swap_in, ans_out, ans_in, pool_out, pool_in, id_out, id_in, tail_out,
    col_order, col_cluster,
    in_sem, send_sem, recv_sem, ma_s, ma_r, mb_s, mb_r, sw_s, sw_r, an_s, an_r,
    po_s, po_r, id_s, id_r, ta_s, ta_r, ready,
):
    me_o = lax.axis_index("owner")
    me_s = lax.axis_index("split")
    y, x = me_o // NX, lax.rem(me_o, NX)
    z, c = me_s // NC, lax.rem(me_s, NC)

    def owner_at(k, sign=1):
        dy, dx = k // NX, k % NX
        if sign < 0:
            dy, dx = NY - dy, NX - dx
        return lax.rem(y + dy, NY) * NX + lax.rem(x + dx, NX)

    def split_at(k, sign=1):
        dc, dz = k // NZ, k % NZ
        if sign < 0:
            dz = NZ - dz
        return lax.rem(z + dz, NZ) * NC + lax.rem(c + dc, NC)

    def remote(src, dst, ssem, rsem, device):
        return pltpu.make_async_remote_copy(
            src_ref=src, dst_ref=dst, send_sem=ssem, recv_sem=rsem,
            device_id=device, device_id_type=MESH,
        )

    clu_in = pltpu.make_async_copy(clu_hbm, clu_v, in_sem.at[0])
    emb_in = pltpu.make_async_copy(emb_hbm, emb, in_sem.at[1])
    ord_in = pltpu.make_async_copy(ord_hbm, ord_v, in_sem.at[2])
    clu_in.start()
    emb_in.start()
    ord_in.start()

    barrier = pltpu.get_barrier_semaphore()
    for k in SPLITS:
        if k:
            pl.semaphore_signal(barrier, inc=1, device_id=(me_o, split_at(k)), device_id_type=MESH)
    for k in STEPS[1:]:
        pl.semaphore_signal(barrier, inc=1, device_id=(owner_at(k), me_s), device_id_type=MESH)

    before = ones_where(iota((ROWS, ROWS), 0) < iota((ROWS, ROWS), 1))
    row, col = iota((BLOCK, BLOCK), 0), iota((BLOCK, BLOCK), 1)
    weave = ones_where(col == ((row >> 1) & 7) * PAIR + (row & 1) * NS + (row >> 4))
    unweave = ones_where(row == ((col >> 1) & 7) * PAIR + (col & 1) * NS + (col >> 4))

    clu_in.wait()
    clu = clu_v[...]
    to_o = clu & (NO - 1)
    to_s = (clu >> 4) & (NS - 1)
    rel_y = ((to_o >> 2) - y) & (NY - 1)
    rel_x = ((to_o & (NX - 1)) - x) & (NX - 1)
    rel_z = ((to_s >> 1) - z) & (NZ - 1)
    rel_c = ((to_s & 1) - c) & 1
    k_o = rel_y * NX + rel_x
    k_s = rel_c * NZ + rel_z
    hot = (k_o * NS + k_s == iota((NO * NS, ROWS), 0)).astype(F32)
    count = dot(hot.astype(BF16), before, (1, 0))
    rank = jnp.sum(hot * count, axis=0, keepdims=True).astype(jnp.int32)
    near = rank < NEAR
    slot[...] = jnp.where(near, k_o * PAIR + rank * NS + k_s, -1)

    hot = jnp.where((rel_z == iota((NZ, ROWS), 0)) & (rank >= NEAR), 1.0, 0.0)
    count = dot(hot.astype(BF16), before, (1, 0))
    place = jnp.sum(hot * count, axis=0, keepdims=True).astype(jnp.int32)
    over = jnp.max(jnp.sum(hot, axis=1, keepdims=True), axis=0, keepdims=True) > POOL
    pool = jnp.where((rank >= NEAR) & (place < POOL), rel_z * POOL + place, -1)
    code = (k_o * NC + rel_c) * TAIL + (rank - NEAR) * NZ + rel_z + 1
    line = iota((8, ROWS), 0)
    parts = jnp.where(line == 0, code >> 6, jnp.where(line == 1, code & 63, 0)).astype(F32).astype(BF16)
    choose = ones_where(pool == iota((POOLED, ROWS), 0))
    got = dot(parts, choose, (1, 1))
    ids = got[0:1] * 64.0 + got[1:2] - 1.0
    for k in range(NZ):
        half = k * POOL // 128
        id_out[k] = ids[:, half * 128 : (half + 1) * 128]

    def normal(rows):
        scale = lax.rsqrt(jnp.sum(rows * rows, axis=1, keepdims=True) + 1e-06)
        return (rows * scale).astype(BF16)

    emb_in.wait()
    pool_out[...] = normal(dot(choose, emb[...], (1, 0)))
    pl.semaphore_wait(barrier, NS - 1 + NO - 1)
    for k in SPLITS:
        if 0 < k < NZ:
            part = pl.ds(k * POOL, POOL)
            remote(pool_out.at[part], pool_in.at[part], po_s, po_r, (me_o, split_at(k))).start()
            remote(id_out.at[k], id_in.at[k], id_s, id_r, (me_o, split_at(k))).start()
    for k in STEPS[1:]:
        pl.semaphore_signal(ready.at[k], inc=1, device_id=(owner_at(k, -1), me_s), device_id_type=MESH)
    pool_in[0:POOL] = pool_out[0:POOL]
    id_in[0] = id_out[0]

    def fill(first):
        steps = STEPS[first : first + 4]
        at = iota((PAIR, ROWS), 0)
        choose = jnp.concatenate([ones_where(slot[...] == b * PAIR + at) for b in steps], axis=0)
        rows = normal(dot(choose, emb[...], (1, 0)))
        for n, b in enumerate(steps):
            mine = rows[n * PAIR : (n + 1) * PAIR]
            parts = jnp.concatenate([mine[:, q * EIGHTH : (q + 1) * EIGHTH] for q in range(8)], axis=0)
            send[b * BLOCK : (b + 1) * BLOCK] = dot(weave, parts, (1, 0)).astype(BF16)

    def ship(b, k):
        part = pl.ds(b * BLOCK + k * LEAF, LEAF)
        if b == 0 and k == 0:
            recv[part] = send[part]
            return
        remote(
            send.at[part], recv.at[part], send_sem.at[b], recv_sem.at[b],
            (owner_at(b), split_at(k)),
        ).start()

    def ship_tail(k):
        part = pl.ds(k * TAIL, TAIL)
        goal = pl.ds(POOL_AT + k * TAIL, TAIL)
        if k == 0:
            keys[goal] = tail_out[part]
            return
        remote(
            tail_out.at[part], keys.at[goal], ta_s, ta_r, (owner_at(k // NC), split_at(k % NC * NZ))
        ).start()

    fill(0)
    for b in STEPS[0:4]:
        if b:
            pl.semaphore_wait(ready.at[b], 1)
        for k in SPLITS:
            ship(b, k)

    onehot[...] = ones_where(k_o * NZ + rel_z == iota((CHIPS, ROWS), 0))
    ord_in.wait()
    orders = ord_v[...]
    code = clu + 1
    parts = jnp.where(
        line == 0, orders >> 12,
        jnp.where(line == 1, (orders >> 6) & 63,
                  jnp.where(line == 2, orders & 63,
                            jnp.where(line == 3, code >> 6,
                                      jnp.where(line == 4, code & 63, 0)))),
    ).astype(F32).astype(BF16)
    by_split = k_s * UNIT + k_o * CAP + rank
    pick = ones_where(by_split == iota((SLOTS, ROWS), 0))
    got = dot(parts, pick, (1, 1))
    slot_order = got[0:1] * 4096.0 + got[1:2] * 64.0 + got[2:3] + jnp.where(over, FLAG, 0.0)
    slot_cluster = got[3:4] * 64.0 + got[4:5] - 1.0
    low = iota((1, 128), 1) < 64
    for p in range(NS // 2):
        a = slot_order[:, p * 128 : (p + 1) * 128]
        b = slot_cluster[:, p * 128 : (p + 1) * 128]
        meta_out[2 * p] = jnp.where(low, a, pltpu.roll(b, 64, 1))
        meta_out[2 * p + 1] = jnp.where(low, pltpu.roll(a, 64, 1), b)
    for k in SPLITS:
        if k:
            remote(meta_out.at[k], meta_mid.at[k], ma_s, ma_r, (me_o, split_at(k))).start()
    meta_mid[0] = meta_out[0]

    fill(4)
    fill(8)
    fill(12)
    for b in STEPS[4:]:
        pl.semaphore_wait(ready.at[b], 1)
    for b in STEPS[4:FIRST]:
        for k in SPLITS:
            ship(b, k)

    some = remote(meta_out.at[pl.ds(1, NS - 1)], meta_mid.at[pl.ds(1, NS - 1)], ma_s, ma_r, (me_o, split_at(1)))
    some.wait_recv()
    for k in STEPS[1:]:
        remote(meta_mid, meta_in.at[k], mb_s, mb_r, (owner_at(k), me_s)).start()
    meta_in[0] = meta_mid[...]
    some.wait_send()
    wide, thin = pl.ds(POOL, POOLED - POOL), pl.ds(1, NZ - 1)
    pools = remote(pool_out.at[wide], pool_in.at[wide], po_s, po_r, (me_o, split_at(1)))
    names = remote(id_out.at[thin], id_in.at[thin], id_s, id_r, (me_o, split_at(1)))
    names.wait_recv()
    part = iota((1, 128), 1) // POOL
    ids = []
    for half in range(POOLED // 128):
        lane_ids = id_in[half * 4]
        for k in range(1, 4):
            lane_ids = jnp.where(part == k, id_in[half * 4 + k], lane_ids)
        ids.append(lane_ids)
    ids = jnp.concatenate(ids, axis=1).astype(jnp.int32)
    choose = ones_where(ids == iota((BLOCKS * TAIL, POOLED), 0))
    pools.wait_recv()
    tail_out[...] = dot(choose, pool_in[...], (1, 0)).astype(BF16)
    rest = [(b, k) for b in STEPS[FIRST:] for k in SPLITS]
    blocks = [b * NC + kc for b in STEPS for kc in range(NC)]
    for n, k in enumerate(blocks):
        ship_tail(k)
        for pair in rest[n * len(rest) // BLOCKS : (n + 1) * len(rest) // BLOCKS]:
            ship(*pair)

    many = remote(meta_in.at[pl.ds(1, NO - 1)], meta_in.at[pl.ds(1, NO - 1)], mb_s, mb_r, (owner_at(1), me_s))
    many.wait_recv()
    widest = jnp.full((NS, 128), -1.0, F32)
    for i, b in enumerate(STEPS):
        lines = meta_in[b].reshape(NS, 128)
        widest = jnp.maximum(widest, lines)
        for r in range(CAP):
            lane = b * CAP + r
            turned = pltpu.roll(lines, 128 - lane, 1) if lane else lines
            if r < NEAR:
                at = i * PAIR + r * NS + (BLOCKS * TAIL if i >= EARLY else 0)
                meta_col[at : at + NS] = turned
            else:
                for kc in range(NC):
                    at = POOL_AT + (b * NC + kc) * TAIL + (r - NEAR) * NZ
                    meta_col[at : at + NZ] = turned[kc * NZ : (kc + 1) * NZ]
    many.wait_send()
    widest = jnp.max(jnp.max(widest, axis=1, keepdims=True), axis=0, keepdims=True)
    turned = meta_col[...].T
    row_order, row_cluster = turned[0:1], turned[64:65]
    col_order[...] = jnp.broadcast_to(meta_col[:, 0:1], (SLOTS, 128))
    col_cluster[...] = jnp.broadcast_to(meta_col[:, 64:65], (SLOTS, 128))


    def take(i):
        b = STEPS[i]
        first = LEAF if b == 0 else 0
        span = pl.ds(b * BLOCK + first, BLOCK - first)
        remote(
            send.at[span], recv.at[span], send_sem.at[b], recv_sem.at[b], (me_o, split_at(1))
        ).wait_recv()
        woven = dot(unweave, recv[b * BLOCK : (b + 1) * BLOCK], (1, 0)).astype(BF16)
        at = i * PAIR + (BLOCKS * TAIL if i >= EARLY else 0)
        for q in range(8):
            keys[at : at + PAIR, q * EIGHTH : (q + 1) * EIGHTH] = woven[q * PAIR : (q + 1) * PAIR]

    def grade(lo, hi):
        scores = dot(keys[0:hi], keys[lo:hi], (1, 1))
        for at in range(lo, hi, 128):
            span = slice(at, at + 128)
            new_order, new_cluster = row_order[:, span], row_cluster[:, span]
            score = jnp.where(col_cluster[0:hi] == new_cluster, scores[:, at - lo : at - lo + 128], -1.0)
            earlier = col_order[0:hi] < new_order
            best_row[:, span] = jnp.max(jnp.where(earlier, score, -1.0), axis=0, keepdims=True)
            later = new_order < col_order[0:hi]
            best_col[0:hi] = jnp.maximum(best_col[0:hi], jnp.where(later, score, -1.0))

    best_col[...] = jnp.full((SLOTS, 128), -1.0, F32)
    for i in range(8):
        take(i)
    grade(0, 8 * PAIR)
    for i in range(8, EARLY):
        take(i)
    grade(8 * PAIR, POOL_AT)
    span = pl.ds(POOL_AT + TAIL, (BLOCKS - 1) * TAIL)
    tails = remote(
        tail_out.at[pl.ds(TAIL, (BLOCKS - 1) * TAIL)], keys.at[span], ta_s, ta_r, (me_o, split_at(1))
    )
    tails.wait_recv()
    grade(POOL_AT, POOL_AT + 256)
    grade(POOL_AT + 256, POOL_AT + 512)
    for i in range(EARLY, NO):
        take(i)
    grade(POOL_AT + 512, SLOTS)

    final = jnp.max(best_col[...], axis=1, keepdims=True)
    final = jnp.maximum(final, jnp.broadcast_to(best_row[...], (128, SLOTS)).T)
    lanes = iota((NZ, 128), 1)
    for i, b in enumerate(STEPS):
        stay = jnp.zeros((NZ, 128), F32)
        leave = jnp.zeros((NZ, 128), F32)
        for r in range(CAP):
            if r < NEAR:
                at = i * PAIR + r * NS + (BLOCKS * TAIL if i >= EARLY else 0)
                gap = NZ
            else:
                at = POOL_AT + b * NC * TAIL + (r - NEAR) * NZ
                gap = TAIL
            stay = jnp.where(lanes == r, final[at : at + NZ], stay)
            leave = jnp.where(lanes == CAP + r, final[at + gap : at + gap + NZ], leave)
        swap_out[b * NZ : (b + 1) * NZ] = leave
        best_col[b * NZ : (b + 1) * NZ] = stay
    swap = remote(swap_out, swap_in, sw_s, sw_r, (me_o, split_at(NZ)))
    swap.start()
    swap.wait_recv()
    both = best_col[0:CHIPS] + swap_in[...]
    ans_out[...] = both.reshape(CHIPS, 1, 128)
    ways = sorted(range(1, CHIPS), key=lambda k: -distance(k // NZ) - min(k % NZ, NZ - k % NZ))
    for k in ways:
        remote(
            ans_out.at[k], ans_in.at[k], an_s, an_r, (owner_at(k // NZ, -1), split_at(k % NZ, -1))
        ).start()
    ans_in[0] = ans_out[0]
    swap.wait_send()
    tails.wait_send()
    pools.wait_send()
    names.wait_send()
    for b in range(NO):
        first = LEAF if b == 0 else 0
        span = pl.ds(b * BLOCK + first, BLOCK - first)
        remote(
            send.at[span], recv.at[span], send_sem.at[b], recv_sem.at[b], (me_o, split_at(1))
        ).wait_send()
    most = pl.ds(1, CHIPS - 1)
    answers = remote(ans_out.at[most], ans_in.at[most], an_s, an_r, (me_o, split_at(1)))
    answers.wait_recv()

    table = ans_in[...].reshape(CHIPS, 128).T[0:8]
    high = table.astype(BF16)
    rest = table - high.astype(F32)
    mid = rest.astype(BF16)
    tiny = (rest - mid.astype(F32)).astype(BF16)
    mine = dot(high, onehot[...], (1, 0)) + dot(mid, onehot[...], (1, 0)) + dot(tiny, onehot[...], (1, 0))
    mine = jnp.sum(jnp.where(line == rel_c * CAP + rank, mine, 0.0), axis=0, keepdims=True)
    out_ref[...] = jnp.where(widest >= FLAG, REDO, mine)
    answers.wait_send()


def common(rows, width):
    return [
        pltpu.VMEM((ROWS, DIM), BF16),
        pltpu.VMEM((1, ROWS), jnp.int32),
        pltpu.VMEM((1, ROWS), jnp.int32),
        pltpu.VMEM((CHIPS, ROWS), BF16),
        pltpu.VMEM((1, ROWS), jnp.int32),
        pltpu.VMEM((rows, width), BF16),
        pltpu.VMEM((rows, width), BF16),
        pltpu.VMEM((SLOTS, DIM), BF16),
        pltpu.VMEM((NS, 1, 128), F32),
        pltpu.VMEM((NS, 1, 128), F32),
        pltpu.VMEM((NO, NS, 1, 128), F32),
        pltpu.VMEM((SLOTS, 128), F32),
        pltpu.VMEM((SLOTS, 128), F32),
        pltpu.VMEM((1, SLOTS), F32),
        pltpu.VMEM((CHIPS, 128), F32),
        pltpu.VMEM((CHIPS, 128), F32),
        pltpu.VMEM((CHIPS, 1, 128), F32),
        pltpu.VMEM((CHIPS, 1, 128), F32),
    ]


def call(kernel, name, number, outs, scratch, args):
    hbm = pl.BlockSpec(memory_space=pltpu.HBM)
    vmem = pl.BlockSpec(memory_space=pltpu.VMEM)
    return pl.pallas_call(
        kernel,
        name=name,
        out_shape=outs,
        in_specs=[hbm] * 3,
        out_specs=[vmem] * len(outs),
        scratch_shapes=scratch,
        compiler_params=pltpu.CompilerParams(
            collective_id=number, has_side_effects=True, vmem_limit_bytes=56 << 20
        ),
        cost_estimate=pl.CostEstimate(
            flops=8 << 30, bytes_accessed=4 << 20, transcendentals=SLOTS
        ),
    )(*args)


def local(embeddings, cluster_id, doc_order):
    args = (embeddings, cluster_id.reshape(1, ROWS), doc_order.reshape(1, ROWS))
    dma = pltpu.SemaphoreType.DMA
    ready = pltpu.SemaphoreType.REGULAR((NO,))
    result = jax.ShapeDtypeStruct((1, ROWS), F32)
    pooled_scratch = common(NO * BLOCK, EIGHTH) + [
        pltpu.VMEM((POOLED, DIM), BF16),
        pltpu.VMEM((POOLED, DIM), BF16),
        pltpu.VMEM((NZ, 1, 128), F32),
        pltpu.VMEM((NZ, 1, 128), F32),
        pltpu.VMEM((BLOCKS * TAIL, DIM), BF16),
        pltpu.VMEM((SLOTS, 128), F32),
        pltpu.VMEM((SLOTS, 128), F32),
        dma((3,)), dma((NO,)), dma((NO,)),
        *[dma] * 14,
        ready,
    ]
    full_scratch = common(NO * BLOCK, QUART) + [
        dma((3,)), dma((NO,)), dma((NO,)),
        *[dma] * 8,
        ready,
    ]
    best = call(pooled_kernel, "pooled", 0, [result], pooled_scratch, args)[0]

    def again(args, best):
        return call(full_kernel, "full", 1, [result], full_scratch, args)[0]

    def keep(args, best):
        return best

    return lax.cond(best[0, 0] > REDO / 2, again, keep, args, best).reshape(ROWS)


def solution(mesh):
    in_specs = (P(("owner", "split"), None), P(("owner", "split")), P(("owner", "split")))
    out_specs = P(("owner", "split"))
    return jax.shard_map(local, mesh=mesh, in_specs=in_specs, out_specs=out_specs, check_vma=False)
```

```python
import jax
import jax.numpy as jnp
from jax import lax
from jax.experimental import pallas as pl
from jax.experimental.pallas import tpu as pltpu
from jax.sharding import PartitionSpec as P

MESH = pl.DeviceIdType.MESH
F32 = jnp.float32
BF16 = jnp.bfloat16

NY, NX, NZ, NC = 4, 4, 8, 2
NO, NS = NY * NX, NZ * NC
CAP = 4
ROWS = 512
DIM = 1024
QUART = DIM // 4
SLOTS = NO * NS * CAP
UNIT = NS * CAP
SLAB = 16
BLOCK = NS * SLAB
CHIPS = NO * NZ

NEAR = 2
PAIR = NS * NEAR
LEAF = 16
EIGHTH = DIM // 8
POOL = 32
POOLED = NZ * POOL
TAIL = NZ * (CAP - NEAR)
BLOCKS = NO * NC
FIRST = 8
EARLY = 12
POOL_AT = EARLY * PAIR
FLAG = 2.0**18
REDO = 4.0


def distance(k):
    dy, dx = divmod(k, NX)
    return min(dy, NY - dy) + min(dx, NX - dx)


STEPS = [0] + sorted(range(1, NO), key=lambda k: -distance(k))
SPLITS = sorted(range(NS), key=lambda k: -min(k % NZ, NZ - k % NZ))


def hops(k):
    return distance(k // NZ) + min(k % NZ, NZ - k % NZ)


WAYS = sorted(range(1, CHIPS), key=lambda k: -hops(k))
FAR = [k for k in WAYS if hops(k) >= 6]


def iota(shape, dim):
    return lax.broadcasted_iota(jnp.int32, shape, dim)


def dot(a, b, contract):
    return lax.dot_general(a, b, ((contract[:1], contract[1:]), ((), ())), preferred_element_type=F32)


def ones_where(mask):
    return mask.astype(F32).astype(BF16)


def full_kernel(
    emb_hbm, clu_hbm, ord_hbm, out_ref,
    emb, clu_v, ord_v, onehot, slot, send, recv, keys, meta_out, meta_mid, meta_in, meta_col,
    best_col, best_row, swap_out, swap_in, ans_out, ans_in,
    in_sem, send_sem, recv_sem, ma_s, ma_r, mb_s, mb_r, sw_s, sw_r, an_s, an_r, ready,
):
    me_o = lax.axis_index("owner")
    me_s = lax.axis_index("split")
    y, x = me_o // NX, lax.rem(me_o, NX)
    z, c = me_s // NC, lax.rem(me_s, NC)

    def owner_at(k, sign=1):
        dy, dx = k // NX, k % NX
        if sign < 0:
            dy, dx = NY - dy, NX - dx
        return lax.rem(y + dy, NY) * NX + lax.rem(x + dx, NX)

    def split_at(k, sign=1):
        dc, dz = k // NZ, k % NZ
        if sign < 0:
            dz = NZ - dz
        return lax.rem(z + dz, NZ) * NC + lax.rem(c + dc, NC)

    def remote(src, dst, ssem, rsem, device):
        return pltpu.make_async_remote_copy(
            src_ref=src, dst_ref=dst, send_sem=ssem, recv_sem=rsem,
            device_id=device, device_id_type=MESH,
        )

    clu_in = pltpu.make_async_copy(clu_hbm, clu_v, in_sem.at[0])
    emb_in = pltpu.make_async_copy(emb_hbm, emb, in_sem.at[1])
    ord_in = pltpu.make_async_copy(ord_hbm, ord_v, in_sem.at[2])
    clu_in.start()
    emb_in.start()
    ord_in.start()

    barrier = pltpu.get_barrier_semaphore()
    for k in SPLITS:
        if k:
            pl.semaphore_signal(barrier, inc=1, device_id=(me_o, split_at(k)), device_id_type=MESH)
    for k in STEPS[1:]:
        pl.semaphore_signal(barrier, inc=1, device_id=(owner_at(k), me_s), device_id_type=MESH)

    before = ones_where(iota((ROWS, ROWS), 0) < iota((ROWS, ROWS), 1))
    row, col = iota((BLOCK, BLOCK), 0), iota((BLOCK, BLOCK), 1)
    weave = ones_where(col == ((row >> 2) & 3) * UNIT + (row & 3) * NS + (row >> 4))
    unweave = ones_where(row == ((col >> 2) & 3) * UNIT + (col & 3) * NS + (col >> 4))

    clu_in.wait()
    clu = clu_v[...]
    to_o = clu & (NO - 1)
    to_s = (clu >> 4) & (NS - 1)
    rel_y = ((to_o >> 2) - y) & (NY - 1)
    rel_x = ((to_o & (NX - 1)) - x) & (NX - 1)
    rel_z = ((to_s >> 1) - z) & (NZ - 1)
    rel_c = ((to_s & 1) - c) & 1
    k_o = rel_y * NX + rel_x
    k_s = rel_c * NZ + rel_z
    hot = (k_o * NS + k_s == iota((NO * NS, ROWS), 0)).astype(F32)
    count = dot(hot.astype(BF16), before, (1, 0))
    rank = jnp.sum(hot * count, axis=0, keepdims=True).astype(jnp.int32)
    slot[...] = k_o * UNIT + rank * NS + k_s

    def fill(b):
        choose = ones_where(slot[...] == b * UNIT + iota((UNIT, ROWS), 0))
        rows = dot(choose, emb[...], (1, 0))
        scale = lax.rsqrt(jnp.sum(rows * rows, axis=1, keepdims=True) + 1e-06)
        rows = (rows * scale).astype(BF16)
        quarters = jnp.concatenate([rows[:, q * QUART : (q + 1) * QUART] for q in range(4)], axis=0)
        send[b * BLOCK : (b + 1) * BLOCK] = dot(weave, quarters, (1, 0)).astype(BF16)

    def ship(b):
        for k in SPLITS:
            part = pl.ds(b * BLOCK + k * SLAB, SLAB)
            if b == 0 and k == 0:
                recv[part] = send[part]
                continue
            remote(
                send.at[part], recv.at[part], send_sem.at[b], recv_sem.at[b],
                (owner_at(b), split_at(k)),
            ).start()

    emb_in.wait()
    fill(0)
    pl.semaphore_wait(barrier, NS - 1 + NO - 1)
    for k in STEPS[1:]:
        pl.semaphore_signal(ready.at[k], inc=1, device_id=(owner_at(k, -1), me_s), device_id_type=MESH)
    ship(0)

    onehot[...] = ones_where(k_o * NZ + rel_z == iota((CHIPS, ROWS), 0))
    ord_in.wait()
    orders = ord_v[...]
    line = iota((8, ROWS), 0)
    code = clu + 1
    parts = jnp.where(
        line == 0, orders >> 12,
        jnp.where(line == 1, (orders >> 6) & 63,
                  jnp.where(line == 2, orders & 63,
                            jnp.where(line == 3, code >> 6,
                                      jnp.where(line == 4, code & 63, 0)))),
    ).astype(F32).astype(BF16)
    by_split = k_s * UNIT + k_o * CAP + rank
    pick = ones_where(by_split == iota((SLOTS, ROWS), 0))
    got = dot(parts, pick, (1, 1))
    slot_order = got[0:1] * 4096.0 + got[1:2] * 64.0 + got[2:3]
    slot_cluster = got[3:4] * 64.0 + got[4:5] - 1.0
    low = iota((1, 128), 1) < 64
    for p in range(NS // 2):
        a = slot_order[:, p * 128 : (p + 1) * 128]
        b = slot_cluster[:, p * 128 : (p + 1) * 128]
        meta_out[2 * p] = jnp.where(low, a, pltpu.roll(b, 64, 1))
        meta_out[2 * p + 1] = jnp.where(low, pltpu.roll(a, 64, 1), b)
    for k in SPLITS:
        if k:
            remote(meta_out.at[k], meta_mid.at[k], ma_s, ma_r, (me_o, split_at(k))).start()
    meta_mid[0] = meta_out[0]

    for b in STEPS[1:]:
        fill(b)
        pl.semaphore_wait(ready.at[b], 1)
        ship(b)

    some = remote(meta_out.at[pl.ds(1, NS - 1)], meta_mid.at[pl.ds(1, NS - 1)], ma_s, ma_r, (me_o, split_at(1)))
    some.wait_recv()
    for k in STEPS[1:]:
        remote(meta_mid, meta_in.at[k], mb_s, mb_r, (owner_at(k), me_s)).start()
    meta_in[0] = meta_mid[...]
    some.wait_send()
    many = remote(meta_in.at[pl.ds(1, NO - 1)], meta_in.at[pl.ds(1, NO - 1)], mb_s, mb_r, (owner_at(1), me_s))
    many.wait_recv()
    for i, b in enumerate(STEPS):
        lines = meta_in[b].reshape(NS, 128)
        for r in range(CAP):
            at = i * UNIT + r * NS
            lane = b * CAP + r
            meta_col[at : at + NS] = pltpu.roll(lines, 128 - lane, 1) if lane else lines
    many.wait_send()
    turned = meta_col[...].T
    row_order, row_cluster = turned[0:1], turned[64:65]

    best_row[...] = jnp.full((1, SLOTS), -1.0, F32)
    step = 2
    for g in range(0, NO, step):
        for i in range(g, g + step):
            b = STEPS[i]
            first = SLAB if b == 0 else 0
            span = pl.ds(b * BLOCK + first, BLOCK - first)
            remote(
                send.at[span], recv.at[span], send_sem.at[b], recv_sem.at[b], (me_o, split_at(1))
            ).wait_recv()
            woven = dot(unweave, recv[b * BLOCK : (b + 1) * BLOCK], (1, 0)).astype(BF16)
            for q in range(4):
                keys[i * UNIT : (i + 1) * UNIT, q * QUART : (q + 1) * QUART] = woven[
                    q * UNIT : (q + 1) * UNIT
                ]
        lo, hi = g * UNIT, (g + step) * UNIT
        score = dot(keys[lo:hi], keys[0:hi], (1, 1))
        new_order, new_cluster = meta_col[lo:hi, 0:1], meta_col[lo:hi, 64:65]
        old_order, old_cluster = row_order[:, :hi], row_cluster[:, :hi]
        score = jnp.where(new_cluster == old_cluster, score, -1.0)
        best = jnp.max(jnp.where(old_order < new_order, score, -1.0), axis=1, keepdims=True)
        best_col[lo:hi] = jnp.broadcast_to(best, (hi - lo, 128))
        best = jnp.max(jnp.where(new_order < old_order, score, -1.0), axis=0, keepdims=True)
        best_row[:, :hi] = jnp.maximum(best_row[:, :hi], best)

    final = jnp.maximum(best_col[...], jnp.broadcast_to(best_row[...], (128, SLOTS)).T)
    lanes = iota((NZ, 128), 1)
    for i, b in enumerate(STEPS):
        stay = jnp.zeros((NZ, 128), F32)
        leave = jnp.zeros((NZ, 128), F32)
        for r in range(CAP):
            at = i * UNIT + r * NS
            stay = jnp.where(lanes == r, final[at : at + NZ], stay)
            leave = jnp.where(lanes == CAP + r, final[at + NZ : at + NS], leave)
        swap_out[b * NZ : (b + 1) * NZ] = leave
        best_col[b * NZ : (b + 1) * NZ] = stay
    swap = remote(swap_out, swap_in, sw_s, sw_r, (me_o, split_at(NZ)))
    swap.start()
    swap.wait_recv()
    both = best_col[0:CHIPS] + swap_in[...]
    ans_out[...] = both.reshape(CHIPS, 1, 128)
    ways = sorted(range(1, CHIPS), key=lambda k: -distance(k // NZ) - min(k % NZ, NZ - k % NZ))
    for k in ways:
        remote(
            ans_out.at[k], ans_in.at[k], an_s, an_r, (owner_at(k // NZ, -1), split_at(k % NZ, -1))
        ).start()
    ans_in[0] = ans_out[0]
    swap.wait_send()
    for b in range(NO):
        first = SLAB if b == 0 else 0
        span = pl.ds(b * BLOCK + first, BLOCK - first)
        remote(
            send.at[span], recv.at[span], send_sem.at[b], recv_sem.at[b], (me_o, split_at(1))
        ).wait_send()
    most = pl.ds(1, CHIPS - 1)
    answers = remote(ans_out.at[most], ans_in.at[most], an_s, an_r, (me_o, split_at(1)))
    answers.wait_recv()

    table = ans_in[...].reshape(CHIPS, 128).T[0:8]
    high = table.astype(BF16)
    rest = table - high.astype(F32)
    mid = rest.astype(BF16)
    tiny = (rest - mid.astype(F32)).astype(BF16)
    mine = dot(high, onehot[...], (1, 0)) + dot(mid, onehot[...], (1, 0)) + dot(tiny, onehot[...], (1, 0))
    out_ref[...] = jnp.sum(jnp.where(line == rel_c * CAP + rank, mine, 0.0), axis=0, keepdims=True)
    answers.wait_send()


def pooled_kernel(
    emb_hbm, clu_ref, ord_ref, out_ref,
    emb, onehot, slot, send, recv, keys, meta_out, meta_mid, meta_in, meta_col,
    best_col, best_row, swap_out, swap_in, ans_out, ans_in, pool_out, pool_in, id_out, id_in, tail_out,
    col_order, col_cluster, far_out, far_in,
    in_sem, send_sem, recv_sem, ma_s, ma_r, mb_s, mb_r, sw_s, sw_r, an_s, an_r,
    po_s, po_r, id_s, id_r, ta_s, ta_r, fa_s, fa_r, ready,
):
    me_o = lax.axis_index("owner")
    me_s = lax.axis_index("split")
    y, x = me_o // NX, lax.rem(me_o, NX)
    z, c = me_s // NC, lax.rem(me_s, NC)

    def owner_at(k, sign=1):
        dy, dx = k // NX, k % NX
        if sign < 0:
            dy, dx = NY - dy, NX - dx
        return lax.rem(y + dy, NY) * NX + lax.rem(x + dx, NX)

    def split_at(k, sign=1):
        dc, dz = k // NZ, k % NZ
        if sign < 0:
            dz = NZ - dz
        return lax.rem(z + dz, NZ) * NC + lax.rem(c + dc, NC)

    def remote(src, dst, ssem, rsem, device):
        return pltpu.make_async_remote_copy(
            src_ref=src, dst_ref=dst, send_sem=ssem, recv_sem=rsem,
            device_id=device, device_id_type=MESH,
        )

    emb_in = pltpu.make_async_copy(emb_hbm, emb, in_sem)
    emb_in.start()

    barrier = pltpu.get_barrier_semaphore()
    for k in SPLITS:
        if k:
            pl.semaphore_signal(barrier, inc=1, device_id=(me_o, split_at(k)), device_id_type=MESH)
    for k in STEPS[1:]:
        pl.semaphore_signal(barrier, inc=1, device_id=(owner_at(k), me_s), device_id_type=MESH)

    before = ones_where(iota((ROWS, ROWS), 0) < iota((ROWS, ROWS), 1))
    row, col = iota((BLOCK, BLOCK), 0), iota((BLOCK, BLOCK), 1)
    weave = ones_where(col == ((row >> 1) & 7) * PAIR + (row & 1) * NS + (row >> 4))
    unweave = ones_where(row == ((col >> 1) & 7) * PAIR + (col & 1) * NS + (col >> 4))

    clu = clu_ref[...]
    to_o = clu & (NO - 1)
    to_s = (clu >> 4) & (NS - 1)
    rel_y = ((to_o >> 2) - y) & (NY - 1)
    rel_x = ((to_o & (NX - 1)) - x) & (NX - 1)
    rel_z = ((to_s >> 1) - z) & (NZ - 1)
    rel_c = ((to_s & 1) - c) & 1
    k_o = rel_y * NX + rel_x
    k_s = rel_c * NZ + rel_z
    hot = (k_o * NS + k_s == iota((NO * NS, ROWS), 0)).astype(F32)
    count = dot(hot.astype(BF16), before, (1, 0))
    rank = jnp.sum(hot * count, axis=0, keepdims=True).astype(jnp.int32)
    near = rank < NEAR
    slot[...] = jnp.where(near, k_o * PAIR + rank * NS + k_s, -1)

    hot = jnp.where((rel_z == iota((NZ, ROWS), 0)) & (rank >= NEAR), 1.0, 0.0)
    count = dot(hot.astype(BF16), before, (1, 0))
    place = jnp.sum(hot * count, axis=0, keepdims=True).astype(jnp.int32)
    over = jnp.max(jnp.sum(hot, axis=1, keepdims=True), axis=0, keepdims=True) > POOL
    pool = jnp.where((rank >= NEAR) & (place < POOL), rel_z * POOL + place, -1)
    code = (k_o * NC + rel_c) * TAIL + (rank - NEAR) * NZ + rel_z + 1
    line = iota((8, ROWS), 0)
    parts = jnp.where(line == 0, code >> 6, jnp.where(line == 1, code & 63, 0)).astype(F32).astype(BF16)
    choose = ones_where(pool == iota((POOLED, ROWS), 0))
    got = dot(parts, choose, (1, 1))
    ids = got[0:1] * 64.0 + got[1:2] - 1.0
    for k in range(NZ):
        half = k * POOL // 128
        id_out[k] = ids[:, half * 128 : (half + 1) * 128]

    def normal(rows):
        scale = lax.rsqrt(jnp.sum(rows * rows, axis=1, keepdims=True) + 1e-06)
        return (rows * scale).astype(BF16)

    emb_in.wait()
    pool_out[...] = normal(dot(choose, emb[...], (1, 0)))
    pl.semaphore_wait(barrier, NS - 1 + NO - 1)
    for k in SPLITS:
        if 0 < k < NZ:
            part = pl.ds(k * POOL, POOL)
            remote(pool_out.at[part], pool_in.at[part], po_s, po_r, (me_o, split_at(k))).start()
            remote(id_out.at[k], id_in.at[k], id_s, id_r, (me_o, split_at(k))).start()
    for k in STEPS[1:]:
        pl.semaphore_signal(ready.at[k], inc=1, device_id=(owner_at(k, -1), me_s), device_id_type=MESH)
    pool_in[0:POOL] = pool_out[0:POOL]
    id_in[0] = id_out[0]

    def fill(first):
        steps = STEPS[first : first + 4]
        at = iota((PAIR, ROWS), 0)
        choose = jnp.concatenate([ones_where(slot[...] == b * PAIR + at) for b in steps], axis=0)
        rows = normal(dot(choose, emb[...], (1, 0)))
        for n, b in enumerate(steps):
            mine = rows[n * PAIR : (n + 1) * PAIR]
            parts = jnp.concatenate([mine[:, q * EIGHTH : (q + 1) * EIGHTH] for q in range(8)], axis=0)
            send[b * BLOCK : (b + 1) * BLOCK] = dot(weave, parts, (1, 0)).astype(BF16)

    def ship(b, k):
        part = pl.ds(b * BLOCK + k * LEAF, LEAF)
        if b == 0 and k == 0:
            recv[part] = send[part]
            return
        remote(
            send.at[part], recv.at[part], send_sem.at[b], recv_sem.at[b],
            (owner_at(b), split_at(k)),
        ).start()

    def ship_tail(k):
        part = pl.ds(k * TAIL, TAIL)
        goal = pl.ds(POOL_AT + k * TAIL, TAIL)
        if k == 0:
            keys[goal] = tail_out[part]
            return
        remote(
            tail_out.at[part], keys.at[goal], ta_s, ta_r, (owner_at(k // NC), split_at(k % NC * NZ))
        ).start()

    onehot[...] = ones_where(k_o * NZ + rel_z == iota((CHIPS, ROWS), 0))
    orders = ord_ref[...]
    code = clu + 1
    parts = jnp.where(
        line == 0, orders >> 12,
        jnp.where(line == 1, (orders >> 6) & 63,
                  jnp.where(line == 2, orders & 63,
                            jnp.where(line == 3, code >> 6,
                                      jnp.where(line == 4, code & 63, 0)))),
    ).astype(F32).astype(BF16)
    by_split = k_s * UNIT + k_o * CAP + rank
    pick = ones_where(by_split == iota((SLOTS, ROWS), 0))
    got = dot(parts, pick, (1, 1))
    slot_order = got[0:1] * 4096.0 + got[1:2] * 64.0 + got[2:3] + jnp.where(over, FLAG, 0.0)
    slot_cluster = got[3:4] * 64.0 + got[4:5] - 1.0
    low = iota((1, 128), 1) < 64
    for p in range(NS // 2):
        a = slot_order[:, p * 128 : (p + 1) * 128]
        b = slot_cluster[:, p * 128 : (p + 1) * 128]
        meta_out[2 * p] = jnp.where(low, a, pltpu.roll(b, 64, 1))
        meta_out[2 * p + 1] = jnp.where(low, pltpu.roll(a, 64, 1), b)
    for k in SPLITS:
        if k:
            remote(meta_out.at[k], meta_mid.at[k], ma_s, ma_r, (me_o, split_at(k))).start()
    meta_mid[0] = meta_out[0]

    fill(0)
    for b in STEPS[0:4]:
        if b:
            pl.semaphore_wait(ready.at[b], 1)
        for k in SPLITS:
            ship(b, k)

    fill(4)
    for b in STEPS[4:FIRST]:
        pl.semaphore_wait(ready.at[b], 1)
        for k in SPLITS:
            ship(b, k)
    fill(8)
    fill(12)
    for b in STEPS[FIRST:]:
        pl.semaphore_wait(ready.at[b], 1)

    wide, thin = pl.ds(POOL, POOLED - POOL), pl.ds(1, NZ - 1)
    pools = remote(pool_out.at[wide], pool_in.at[wide], po_s, po_r, (me_o, split_at(1)))
    names = remote(id_out.at[thin], id_in.at[thin], id_s, id_r, (me_o, split_at(1)))
    names.wait_recv()
    part = iota((1, 128), 1) // POOL
    ids = []
    for half in range(POOLED // 128):
        lane_ids = id_in[half * 4]
        for k in range(1, 4):
            lane_ids = jnp.where(part == k, id_in[half * 4 + k], lane_ids)
        ids.append(lane_ids)
    ids = jnp.concatenate(ids, axis=1).astype(jnp.int32)
    choose = ones_where(ids == iota((BLOCKS * TAIL, POOLED), 0))
    pools.wait_recv()
    tail_out[...] = dot(choose, pool_in[...], (1, 0)).astype(BF16)

    some = remote(meta_out.at[pl.ds(1, NS - 1)], meta_mid.at[pl.ds(1, NS - 1)], ma_s, ma_r, (me_o, split_at(1)))
    some.wait_recv()
    for k in STEPS[1:]:
        remote(meta_mid, meta_in.at[k], mb_s, mb_r, (owner_at(k), me_s)).start()
    meta_in[0] = meta_mid[...]
    some.wait_send()
    rest = [(b, k) for b in STEPS[FIRST:] for k in SPLITS]
    blocks = [b * NC + kc for b in STEPS for kc in range(NC)]
    for n, k in enumerate(blocks):
        ship_tail(k)
        for pair in rest[n * 3 : (n + 1) * 3]:
            ship(*pair)
    for pair in rest[BLOCKS * 3 :]:
        ship(*pair)

    many = remote(meta_in.at[pl.ds(1, NO - 1)], meta_in.at[pl.ds(1, NO - 1)], mb_s, mb_r, (owner_at(1), me_s))
    many.wait_recv()
    widest = jnp.full((NS, 128), -1.0, F32)
    for i, b in enumerate(STEPS):
        lines = meta_in[b].reshape(NS, 128)
        widest = jnp.maximum(widest, lines)
        for r in range(CAP):
            lane = b * CAP + r
            turned = pltpu.roll(lines, 128 - lane, 1) if lane else lines
            if r < NEAR:
                at = i * PAIR + r * NS + (BLOCKS * TAIL if i >= EARLY else 0)
                meta_col[at : at + NS] = turned
            else:
                for kc in range(NC):
                    at = POOL_AT + (b * NC + kc) * TAIL + (r - NEAR) * NZ
                    meta_col[at : at + NZ] = turned[kc * NZ : (kc + 1) * NZ]
    many.wait_send()
    widest = jnp.max(jnp.max(widest, axis=1, keepdims=True), axis=0, keepdims=True)
    turned = meta_col[...].T
    row_order, row_cluster = turned[0:1], turned[64:65]
    col_order[...] = jnp.broadcast_to(meta_col[:, 0:1], (SLOTS, 128))
    col_cluster[...] = jnp.broadcast_to(meta_col[:, 64:65], (SLOTS, 128))


    def take(i):
        b = STEPS[i]
        first = LEAF if b == 0 else 0
        span = pl.ds(b * BLOCK + first, BLOCK - first)
        remote(
            send.at[span], recv.at[span], send_sem.at[b], recv_sem.at[b], (me_o, split_at(1))
        ).wait_recv()
        woven = dot(unweave, recv[b * BLOCK : (b + 1) * BLOCK], (1, 0)).astype(BF16)
        at = i * PAIR + (BLOCKS * TAIL if i >= EARLY else 0)
        for q in range(8):
            keys[at : at + PAIR, q * EIGHTH : (q + 1) * EIGHTH] = woven[q * PAIR : (q + 1) * PAIR]

    def grade(lo, hi):
        scores = dot(keys[0:hi], keys[lo:hi], (1, 1))
        for at in range(lo, hi, 128):
            span = slice(at, at + 128)
            new_order, new_cluster = row_order[:, span], row_cluster[:, span]
            score = jnp.where(col_cluster[0:hi] == new_cluster, scores[:, at - lo : at - lo + 128], -1.0)
            earlier = col_order[0:hi] < new_order
            best_row[:, span] = jnp.max(jnp.where(earlier, score, -1.0), axis=0, keepdims=True)
            later = new_order < col_order[0:hi]
            best_col[0:hi] = jnp.maximum(best_col[0:hi], jnp.where(later, score, -1.0))

    best_col[...] = jnp.full((SLOTS, 128), -1.0, F32)
    for i in range(8):
        take(i)
    grade(0, 8 * PAIR)
    for i in range(8, EARLY):
        take(i)
    grade(8 * PAIR, POOL_AT)
    span = pl.ds(POOL_AT + TAIL, (BLOCKS - 1) * TAIL)
    tails = remote(
        tail_out.at[pl.ds(TAIL, (BLOCKS - 1) * TAIL)], keys.at[span], ta_s, ta_r, (me_o, split_at(1))
    )
    tails.wait_recv()
    grade(POOL_AT, POOL_AT + 256)
    grade(POOL_AT + 256, POOL_AT + 512)
    for i in range(EARLY, NO):
        take(i)
    grade(POOL_AT + 512, SLOTS)

    final = jnp.max(best_col[...], axis=1, keepdims=True)
    final = jnp.maximum(final, jnp.broadcast_to(best_row[...], (128, SLOTS)).T)
    lanes = iota((NZ, 128), 1)
    for i, b in enumerate(STEPS):
        stay = jnp.zeros((NZ, 128), F32)
        leave = jnp.zeros((NZ, 128), F32)
        for r in range(CAP):
            if r < NEAR:
                at = i * PAIR + r * NS + (BLOCKS * TAIL if i >= EARLY else 0)
                gap = NZ
            else:
                at = POOL_AT + b * NC * TAIL + (r - NEAR) * NZ
                gap = TAIL
            stay = jnp.where(lanes == r, final[at : at + NZ], stay)
            leave = jnp.where(lanes == CAP + r, final[at + gap : at + gap + NZ], leave)
        swap_out[b * NZ : (b + 1) * NZ] = leave
        best_col[b * NZ : (b + 1) * NZ] = stay
    swap = remote(swap_out, swap_in, sw_s, sw_r, (me_o, split_at(NZ)))
    swap.start()
    for n, k in enumerate(FAR):
        far_out[n] = best_col[k : k + 1]
        far_out[len(FAR) + n] = swap_out[k : k + 1]
    for n, k in enumerate(FAR):
        ko, dz = k // NZ, k % NZ
        remote(
            far_out.at[n], ans_in.at[k], fa_s, an_r, (owner_at(ko, -1), split_at(dz, -1))
        ).start()
        remote(
            far_out.at[len(FAR) + n], far_in.at[n], fa_s, fa_r, (owner_at(ko, -1), split_at(NZ + dz, -1))
        ).start()
    swap.wait_recv()
    both = best_col[0:CHIPS] + swap_in[...]
    ans_out[...] = both.reshape(CHIPS, 1, 128)
    for k in WAYS[len(FAR) :]:
        remote(
            ans_out.at[k], ans_in.at[k], an_s, an_r, (owner_at(k // NZ, -1), split_at(k % NZ, -1))
        ).start()
    ans_in[0] = ans_out[0]
    swap.wait_send()
    tails.wait_send()
    pools.wait_send()
    names.wait_send()
    for b in range(NO):
        first = LEAF if b == 0 else 0
        span = pl.ds(b * BLOCK + first, BLOCK - first)
        remote(
            send.at[span], recv.at[span], send_sem.at[b], recv_sem.at[b], (me_o, split_at(1))
        ).wait_send()
    most, less = pl.ds(1, CHIPS - 1), pl.ds(1, CHIPS - 1 - len(FAR))
    remote(ans_out.at[less], ans_in.at[less], an_s, an_r, (me_o, split_at(1))).wait_send()
    alone = pl.ds(0, len(FAR))
    remote(far_out, far_out, fa_s, fa_r, (me_o, split_at(1))).wait_send()
    remote(ans_out.at[most], ans_in.at[most], an_s, an_r, (me_o, split_at(1))).wait_recv()
    remote(far_out.at[alone], far_in.at[alone], fa_s, fa_r, (me_o, split_at(1))).wait_recv()
    for n, k in enumerate(FAR):
        ans_in[k] = ans_in[k] + far_in[n]

    table = ans_in[...].reshape(CHIPS, 128).T[0:8]
    high = table.astype(BF16)
    rest = table - high.astype(F32)
    mid = rest.astype(BF16)
    tiny = (rest - mid.astype(F32)).astype(BF16)
    mine = dot(high, onehot[...], (1, 0)) + dot(mid, onehot[...], (1, 0)) + dot(tiny, onehot[...], (1, 0))
    mine = jnp.sum(jnp.where(line == rel_c * CAP + rank, mine, 0.0), axis=0, keepdims=True)
    out_ref[...] = jnp.where(widest >= FLAG, REDO, mine)


def common(rows, width):
    return [
        pltpu.VMEM((CHIPS, ROWS), BF16),
        pltpu.VMEM((1, ROWS), jnp.int32),
        pltpu.VMEM((rows, width), BF16),
        pltpu.VMEM((rows, width), BF16),
        pltpu.VMEM((SLOTS, DIM), BF16),
        pltpu.VMEM((NS, 1, 128), F32),
        pltpu.VMEM((NS, 1, 128), F32),
        pltpu.VMEM((NO, NS, 1, 128), F32),
        pltpu.VMEM((SLOTS, 128), F32),
        pltpu.VMEM((SLOTS, 128), F32),
        pltpu.VMEM((1, SLOTS), F32),
        pltpu.VMEM((CHIPS, 128), F32),
        pltpu.VMEM((CHIPS, 128), F32),
        pltpu.VMEM((CHIPS, 1, 128), F32),
        pltpu.VMEM((CHIPS, 1, 128), F32),
    ]


def call(kernel, name, number, out, small, scratch, args):
    hbm = pl.BlockSpec(memory_space=pltpu.HBM)
    vmem = pl.BlockSpec(memory_space=pltpu.VMEM)
    return pl.pallas_call(
        kernel,
        name=name,
        out_shape=out,
        in_specs=[hbm] + [vmem if small else hbm] * 2,
        out_specs=vmem,
        scratch_shapes=scratch,
        compiler_params=pltpu.CompilerParams(
            collective_id=number, has_side_effects=True, vmem_limit_bytes=56 << 20
        ),
        cost_estimate=pl.CostEstimate(
            flops=8 << 30, bytes_accessed=4 << 20, transcendentals=SLOTS
        ),
    )(*args)


def local(embeddings, cluster_id, doc_order):
    args = (embeddings, cluster_id.reshape(1, ROWS), doc_order.reshape(1, ROWS))
    dma = pltpu.SemaphoreType.DMA
    ready = pltpu.SemaphoreType.REGULAR((NO,))
    result = jax.ShapeDtypeStruct((1, ROWS), F32)
    pooled_scratch = [pltpu.VMEM((ROWS, DIM), BF16)] + common(NO * BLOCK, EIGHTH) + [
        pltpu.VMEM((POOLED, DIM), BF16),
        pltpu.VMEM((POOLED, DIM), BF16),
        pltpu.VMEM((NZ, 1, 128), F32),
        pltpu.VMEM((NZ, 1, 128), F32),
        pltpu.VMEM((BLOCKS * TAIL, DIM), BF16),
        pltpu.VMEM((SLOTS, 128), F32),
        pltpu.VMEM((SLOTS, 128), F32),
        pltpu.VMEM((2 * len(FAR), 1, 128), F32),
        pltpu.VMEM((len(FAR), 1, 128), F32),
        dma, dma((NO,)), dma((NO,)),
        *[dma] * 16,
        ready,
    ]
    line = pltpu.VMEM((1, ROWS), jnp.int32)
    full_scratch = [pltpu.VMEM((ROWS, DIM), BF16), line, line] + common(NO * BLOCK, QUART) + [
        dma((3,)), dma((NO,)), dma((NO,)),
        *[dma] * 8,
        ready,
    ]
    best = call(pooled_kernel, "pooled", 0, result, True, pooled_scratch, args)

    def again(args, best):
        return call(full_kernel, "full", 1, result, False, full_scratch, args)

    def keep(args, best):
        return best

    return lax.cond(best[0, 0] > REDO / 2, again, keep, args, best).reshape(ROWS)


def solution(mesh):
    in_specs = (P(("owner", "split"), None), P(("owner", "split")), P(("owner", "split")))
    out_specs = P(("owner", "split"))
    return jax.shard_map(local, mesh=mesh, in_specs=in_specs, out_specs=out_specs, check_vma=False)
```

```python
import jax
import jax.numpy as jnp
from jax import lax
from jax.experimental import pallas as pl
from jax.experimental.pallas import tpu as pltpu
from jax.sharding import PartitionSpec as P

MESH = pl.DeviceIdType.MESH
F32 = jnp.float32
BF16 = jnp.bfloat16

NY, NX, NZ, NC = 4, 4, 8, 2
NO, NS = NY * NX, NZ * NC
CAP = 4
ROWS = 512
DIM = 1024
QUART = DIM // 4
SLOTS = NO * NS * CAP
UNIT = NS * CAP
SLAB = 16
BLOCK = NS * SLAB
CHIPS = NO * NZ

NEAR = 2
PAIR = NS * NEAR
LEAF = 16
EIGHTH = DIM // 8
POOL = 32
POOLED = NZ * POOL
TAIL = NZ * (CAP - NEAR)
BLOCKS = NO * NC
FIRST = 8
EARLY = 12
POOL_AT = EARLY * PAIR
FLAG = 2.0**18
REDO = 4.0


def distance(k):
    dy, dx = divmod(k, NX)
    return min(dy, NY - dy) + min(dx, NX - dx)


STEPS = [0] + sorted(range(1, NO), key=lambda k: -distance(k))
SPLITS = sorted(range(NS), key=lambda k: -min(k % NZ, NZ - k % NZ))


def hops(k):
    return distance(k // NZ) + min(k % NZ, NZ - k % NZ)


WAYS = sorted(range(1, CHIPS), key=lambda k: -hops(k))
FAR = [k for k in WAYS if hops(k) >= 6]


def iota(shape, dim):
    return lax.broadcasted_iota(jnp.int32, shape, dim)


def dot(a, b, contract):
    return lax.dot_general(a, b, ((contract[:1], contract[1:]), ((), ())), preferred_element_type=F32)


def ones_where(mask):
    return mask.astype(F32).astype(BF16)


def full_kernel(
    emb_hbm, clu_hbm, ord_hbm, out_ref,
    emb, clu_v, ord_v, onehot, slot, send, recv, keys, meta_out, meta_mid, meta_in, meta_col,
    best_col, best_row, swap_out, swap_in, ans_out, ans_in,
    in_sem, send_sem, recv_sem, ma_s, ma_r, mb_s, mb_r, sw_s, sw_r, an_s, an_r, ready,
):
    me_o = lax.axis_index("owner")
    me_s = lax.axis_index("split")
    y, x = me_o // NX, lax.rem(me_o, NX)
    z, c = me_s // NC, lax.rem(me_s, NC)

    def owner_at(k, sign=1):
        dy, dx = k // NX, k % NX
        if sign < 0:
            dy, dx = NY - dy, NX - dx
        return lax.rem(y + dy, NY) * NX + lax.rem(x + dx, NX)

    def split_at(k, sign=1):
        dc, dz = k // NZ, k % NZ
        if sign < 0:
            dz = NZ - dz
        return lax.rem(z + dz, NZ) * NC + lax.rem(c + dc, NC)

    def remote(src, dst, ssem, rsem, device):
        return pltpu.make_async_remote_copy(
            src_ref=src, dst_ref=dst, send_sem=ssem, recv_sem=rsem,
            device_id=device, device_id_type=MESH,
        )

    clu_in = pltpu.make_async_copy(clu_hbm, clu_v, in_sem.at[0])
    emb_in = pltpu.make_async_copy(emb_hbm, emb, in_sem.at[1])
    ord_in = pltpu.make_async_copy(ord_hbm, ord_v, in_sem.at[2])
    clu_in.start()
    emb_in.start()
    ord_in.start()

    barrier = pltpu.get_barrier_semaphore()
    for k in SPLITS:
        if k:
            pl.semaphore_signal(barrier, inc=1, device_id=(me_o, split_at(k)), device_id_type=MESH)
    for k in STEPS[1:]:
        pl.semaphore_signal(barrier, inc=1, device_id=(owner_at(k), me_s), device_id_type=MESH)

    before = ones_where(iota((ROWS, ROWS), 0) < iota((ROWS, ROWS), 1))
    row, col = iota((BLOCK, BLOCK), 0), iota((BLOCK, BLOCK), 1)
    weave = ones_where(col == ((row >> 2) & 3) * UNIT + (row & 3) * NS + (row >> 4))
    unweave = ones_where(row == ((col >> 2) & 3) * UNIT + (col & 3) * NS + (col >> 4))

    clu_in.wait()
    clu = clu_v[...]
    to_o = clu & (NO - 1)
    to_s = (clu >> 4) & (NS - 1)
    rel_y = ((to_o >> 2) - y) & (NY - 1)
    rel_x = ((to_o & (NX - 1)) - x) & (NX - 1)
    rel_z = ((to_s >> 1) - z) & (NZ - 1)
    rel_c = ((to_s & 1) - c) & 1
    k_o = rel_y * NX + rel_x
    k_s = rel_c * NZ + rel_z
    hot = (k_o * NS + k_s == iota((NO * NS, ROWS), 0)).astype(F32)
    count = dot(hot.astype(BF16), before, (1, 0))
    rank = jnp.sum(hot * count, axis=0, keepdims=True).astype(jnp.int32)
    slot[...] = k_o * UNIT + rank * NS + k_s

    def fill(b):
        choose = ones_where(slot[...] == b * UNIT + iota((UNIT, ROWS), 0))
        rows = dot(choose, emb[...], (1, 0))
        scale = lax.rsqrt(jnp.sum(rows * rows, axis=1, keepdims=True) + 1e-06)
        rows = (rows * scale).astype(BF16)
        quarters = jnp.concatenate([rows[:, q * QUART : (q + 1) * QUART] for q in range(4)], axis=0)
        send[b * BLOCK : (b + 1) * BLOCK] = dot(weave, quarters, (1, 0)).astype(BF16)

    def ship(b):
        for k in SPLITS:
            part = pl.ds(b * BLOCK + k * SLAB, SLAB)
            if b == 0 and k == 0:
                recv[part] = send[part]
                continue
            remote(
                send.at[part], recv.at[part], send_sem.at[b], recv_sem.at[b],
                (owner_at(b), split_at(k)),
            ).start()

    emb_in.wait()
    fill(0)
    pl.semaphore_wait(barrier, NS - 1 + NO - 1)
    for k in STEPS[1:]:
        pl.semaphore_signal(ready.at[k], inc=1, device_id=(owner_at(k, -1), me_s), device_id_type=MESH)
    ship(0)

    onehot[...] = ones_where(k_o * NZ + rel_z == iota((CHIPS, ROWS), 0))
    ord_in.wait()
    orders = ord_v[...]
    line = iota((8, ROWS), 0)
    code = clu + 1
    parts = jnp.where(
        line == 0, orders >> 12,
        jnp.where(line == 1, (orders >> 6) & 63,
                  jnp.where(line == 2, orders & 63,
                            jnp.where(line == 3, code >> 6,
                                      jnp.where(line == 4, code & 63, 0)))),
    ).astype(F32).astype(BF16)
    by_split = k_s * UNIT + k_o * CAP + rank
    pick = ones_where(by_split == iota((SLOTS, ROWS), 0))
    got = dot(parts, pick, (1, 1))
    slot_order = got[0:1] * 4096.0 + got[1:2] * 64.0 + got[2:3]
    slot_cluster = got[3:4] * 64.0 + got[4:5] - 1.0
    low = iota((1, 128), 1) < 64
    for p in range(NS // 2):
        a = slot_order[:, p * 128 : (p + 1) * 128]
        b = slot_cluster[:, p * 128 : (p + 1) * 128]
        meta_out[2 * p] = jnp.where(low, a, pltpu.roll(b, 64, 1))
        meta_out[2 * p + 1] = jnp.where(low, pltpu.roll(a, 64, 1), b)
    for k in SPLITS:
        if k:
            remote(meta_out.at[k], meta_mid.at[k], ma_s, ma_r, (me_o, split_at(k))).start()
    meta_mid[0] = meta_out[0]

    for b in STEPS[1:]:
        fill(b)
        pl.semaphore_wait(ready.at[b], 1)
        ship(b)

    some = remote(meta_out.at[pl.ds(1, NS - 1)], meta_mid.at[pl.ds(1, NS - 1)], ma_s, ma_r, (me_o, split_at(1)))
    some.wait_recv()
    for k in STEPS[1:]:
        remote(meta_mid, meta_in.at[k], mb_s, mb_r, (owner_at(k), me_s)).start()
    meta_in[0] = meta_mid[...]
    some.wait_send()
    many = remote(meta_in.at[pl.ds(1, NO - 1)], meta_in.at[pl.ds(1, NO - 1)], mb_s, mb_r, (owner_at(1), me_s))
    many.wait_recv()
    for i, b in enumerate(STEPS):
        lines = meta_in[b].reshape(NS, 128)
        for r in range(CAP):
            at = i * UNIT + r * NS
            lane = b * CAP + r
            meta_col[at : at + NS] = pltpu.roll(lines, 128 - lane, 1) if lane else lines
    many.wait_send()
    turned = meta_col[...].T
    row_order, row_cluster = turned[0:1], turned[64:65]

    best_row[...] = jnp.full((1, SLOTS), -1.0, F32)
    step = 2
    for g in range(0, NO, step):
        for i in range(g, g + step):
            b = STEPS[i]
            first = SLAB if b == 0 else 0
            span = pl.ds(b * BLOCK + first, BLOCK - first)
            remote(
                send.at[span], recv.at[span], send_sem.at[b], recv_sem.at[b], (me_o, split_at(1))
            ).wait_recv()
            woven = dot(unweave, recv[b * BLOCK : (b + 1) * BLOCK], (1, 0)).astype(BF16)
            for q in range(4):
                keys[i * UNIT : (i + 1) * UNIT, q * QUART : (q + 1) * QUART] = woven[
                    q * UNIT : (q + 1) * UNIT
                ]
        lo, hi = g * UNIT, (g + step) * UNIT
        score = dot(keys[lo:hi], keys[0:hi], (1, 1))
        new_order, new_cluster = meta_col[lo:hi, 0:1], meta_col[lo:hi, 64:65]
        old_order, old_cluster = row_order[:, :hi], row_cluster[:, :hi]
        score = jnp.where(new_cluster == old_cluster, score, -1.0)
        best = jnp.max(jnp.where(old_order < new_order, score, -1.0), axis=1, keepdims=True)
        best_col[lo:hi] = jnp.broadcast_to(best, (hi - lo, 128))
        best = jnp.max(jnp.where(new_order < old_order, score, -1.0), axis=0, keepdims=True)
        best_row[:, :hi] = jnp.maximum(best_row[:, :hi], best)

    final = jnp.maximum(best_col[...], jnp.broadcast_to(best_row[...], (128, SLOTS)).T)
    lanes = iota((NZ, 128), 1)
    for i, b in enumerate(STEPS):
        stay = jnp.zeros((NZ, 128), F32)
        leave = jnp.zeros((NZ, 128), F32)
        for r in range(CAP):
            at = i * UNIT + r * NS
            stay = jnp.where(lanes == r, final[at : at + NZ], stay)
            leave = jnp.where(lanes == CAP + r, final[at + NZ : at + NS], leave)
        swap_out[b * NZ : (b + 1) * NZ] = leave
        best_col[b * NZ : (b + 1) * NZ] = stay
    swap = remote(swap_out, swap_in, sw_s, sw_r, (me_o, split_at(NZ)))
    swap.start()
    swap.wait_recv()
    both = best_col[0:CHIPS] + swap_in[...]
    ans_out[...] = both.reshape(CHIPS, 1, 128)
    ways = sorted(range(1, CHIPS), key=lambda k: -distance(k // NZ) - min(k % NZ, NZ - k % NZ))
    for k in ways:
        remote(
            ans_out.at[k], ans_in.at[k], an_s, an_r, (owner_at(k // NZ, -1), split_at(k % NZ, -1))
        ).start()
    ans_in[0] = ans_out[0]
    swap.wait_send()
    for b in range(NO):
        first = SLAB if b == 0 else 0
        span = pl.ds(b * BLOCK + first, BLOCK - first)
        remote(
            send.at[span], recv.at[span], send_sem.at[b], recv_sem.at[b], (me_o, split_at(1))
        ).wait_send()
    most = pl.ds(1, CHIPS - 1)
    answers = remote(ans_out.at[most], ans_in.at[most], an_s, an_r, (me_o, split_at(1)))
    answers.wait_recv()

    table = ans_in[...].reshape(CHIPS, 128).T[0:8]
    high = table.astype(BF16)
    rest = table - high.astype(F32)
    mid = rest.astype(BF16)
    tiny = (rest - mid.astype(F32)).astype(BF16)
    mine = dot(high, onehot[...], (1, 0)) + dot(mid, onehot[...], (1, 0)) + dot(tiny, onehot[...], (1, 0))
    out_ref[...] = jnp.sum(jnp.where(line == rel_c * CAP + rank, mine, 0.0), axis=0, keepdims=True)
    answers.wait_send()


def pooled_kernel(
    emb_hbm, clu_ref, ord_ref, out_ref,
    emb, onehot, slot, send, recv, keys, meta_out, meta_mid, meta_in, meta_col,
    best_col, best_row, swap_out, swap_in, ans_out, ans_in, pool_out, pool_in, id_out, id_in, tail_out,
    col_order, col_cluster, far_out, far_in,
    in_sem, send_sem, recv_sem, ma_s, ma_r, mb_s, mb_r, sw_s, sw_r, an_s, an_r,
    po_s, po_r, id_s, id_r, ta_s, ta_r, fa_s, fa_r, ready,
):
    me_o = lax.axis_index("owner")
    me_s = lax.axis_index("split")
    y, x = me_o // NX, lax.rem(me_o, NX)
    z, c = me_s // NC, lax.rem(me_s, NC)

    def owner_at(k, sign=1):
        dy, dx = k // NX, k % NX
        if sign < 0:
            dy, dx = NY - dy, NX - dx
        return lax.rem(y + dy, NY) * NX + lax.rem(x + dx, NX)

    def split_at(k, sign=1):
        dc, dz = k // NZ, k % NZ
        if sign < 0:
            dz = NZ - dz
        return lax.rem(z + dz, NZ) * NC + lax.rem(c + dc, NC)

    def remote(src, dst, ssem, rsem, device):
        return pltpu.make_async_remote_copy(
            src_ref=src, dst_ref=dst, send_sem=ssem, recv_sem=rsem,
            device_id=device, device_id_type=MESH,
        )

    emb_in = pltpu.make_async_copy(emb_hbm, emb, in_sem)
    emb_in.start()

    barrier = pltpu.get_barrier_semaphore()
    for k in SPLITS:
        if k:
            pl.semaphore_signal(barrier, inc=1, device_id=(me_o, split_at(k)), device_id_type=MESH)
    for k in STEPS[1:]:
        pl.semaphore_signal(barrier, inc=1, device_id=(owner_at(k), me_s), device_id_type=MESH)

    before = ones_where(iota((ROWS, ROWS), 0) < iota((ROWS, ROWS), 1))

    clu = clu_ref[...]
    to_o = clu & (NO - 1)
    to_s = (clu >> 4) & (NS - 1)
    rel_y = ((to_o >> 2) - y) & (NY - 1)
    rel_x = ((to_o & (NX - 1)) - x) & (NX - 1)
    rel_z = ((to_s >> 1) - z) & (NZ - 1)
    rel_c = ((to_s & 1) - c) & 1
    k_o = rel_y * NX + rel_x
    k_s = rel_c * NZ + rel_z
    hot = (k_o * NS + k_s == iota((NO * NS, ROWS), 0)).astype(F32)
    count = dot(hot.astype(BF16), before, (1, 0))
    rank = jnp.sum(hot * count, axis=0, keepdims=True).astype(jnp.int32)
    near = rank < NEAR
    slot[...] = jnp.where(near, k_o * PAIR + rank * NS + k_s, -1)

    hot = jnp.where((rel_z == iota((NZ, ROWS), 0)) & (rank >= NEAR), 1.0, 0.0)
    count = dot(hot.astype(BF16), before, (1, 0))
    place = jnp.sum(hot * count, axis=0, keepdims=True).astype(jnp.int32)
    over = jnp.max(jnp.sum(hot, axis=1, keepdims=True), axis=0, keepdims=True) > POOL
    pool = jnp.where((rank >= NEAR) & (place < POOL), rel_z * POOL + place, -1)
    code = (k_o * NC + rel_c) * TAIL + (rank - NEAR) * NZ + rel_z + 1
    line = iota((8, ROWS), 0)
    parts = jnp.where(line == 0, code >> 6, jnp.where(line == 1, code & 63, 0)).astype(F32).astype(BF16)
    choose = ones_where(pool == iota((POOLED, ROWS), 0))
    got = dot(parts, choose, (1, 1))
    ids = got[0:1] * 64.0 + got[1:2] - 1.0
    for k in range(NZ):
        half = k * POOL // 128
        id_out[k] = ids[:, half * 128 : (half + 1) * 128]

    def normal(rows):
        scale = lax.rsqrt(jnp.sum(rows * rows, axis=1, keepdims=True) + 1e-06)
        return (rows * scale).astype(BF16)

    emb_in.wait()
    pool_out[...] = normal(dot(choose, emb[...], (1, 0)))
    pl.semaphore_wait(barrier, NS - 1 + NO - 1)
    for k in SPLITS:
        if 0 < k < NZ:
            part = pl.ds(k * POOL, POOL)
            remote(pool_out.at[part], pool_in.at[part], po_s, po_r, (me_o, split_at(k))).start()
            remote(id_out.at[k], id_in.at[k], id_s, id_r, (me_o, split_at(k))).start()
    for k in STEPS[1:]:
        pl.semaphore_signal(ready.at[k], inc=1, device_id=(owner_at(k, -1), me_s), device_id_type=MESH)
    pool_in[0:POOL] = pool_out[0:POOL]
    id_in[0] = id_out[0]

    row, col = iota((BLOCK, BLOCK), 0), iota((BLOCK, BLOCK), 1)
    weave = ones_where(col == ((row >> 1) & 7) * PAIR + (row & 1) * NS + (row >> 4))
    unweave = ones_where(row == ((col >> 1) & 7) * PAIR + (col & 1) * NS + (col >> 4))

    def fill(first):
        steps = STEPS[first : first + 4]
        at = iota((PAIR, ROWS), 0)
        choose = jnp.concatenate([ones_where(slot[...] == b * PAIR + at) for b in steps], axis=0)
        rows = normal(dot(choose, emb[...], (1, 0)))
        for n, b in enumerate(steps):
            mine = rows[n * PAIR : (n + 1) * PAIR]
            parts = jnp.concatenate([mine[:, q * EIGHTH : (q + 1) * EIGHTH] for q in range(8)], axis=0)
            send[b * BLOCK : (b + 1) * BLOCK] = dot(weave, parts, (1, 0)).astype(BF16)

    def ship(b, k):
        part = pl.ds(b * BLOCK + k * LEAF, LEAF)
        if b == 0 and k == 0:
            recv[part] = send[part]
            return
        remote(
            send.at[part], recv.at[part], send_sem.at[b], recv_sem.at[b],
            (owner_at(b), split_at(k)),
        ).start()

    def ship_tail(k):
        part = pl.ds(k * TAIL, TAIL)
        goal = pl.ds(POOL_AT + k * TAIL, TAIL)
        if k == 0:
            keys[goal] = tail_out[part]
            return
        remote(
            tail_out.at[part], keys.at[goal], ta_s, ta_r, (owner_at(k // NC), split_at(k % NC * NZ))
        ).start()

    onehot[...] = ones_where(k_o * NZ + rel_z == iota((CHIPS, ROWS), 0))
    orders = ord_ref[...]
    code = clu + 1
    parts = jnp.where(
        line == 0, orders >> 12,
        jnp.where(line == 1, (orders >> 6) & 63,
                  jnp.where(line == 2, orders & 63,
                            jnp.where(line == 3, code >> 6,
                                      jnp.where(line == 4, code & 63, 0)))),
    ).astype(F32).astype(BF16)
    by_split = k_s * UNIT + k_o * CAP + rank
    pick = ones_where(by_split == iota((SLOTS, ROWS), 0))
    got = dot(parts, pick, (1, 1))
    slot_order = got[0:1] * 4096.0 + got[1:2] * 64.0 + got[2:3] + jnp.where(over, FLAG, 0.0)
    slot_cluster = got[3:4] * 64.0 + got[4:5] - 1.0
    low = iota((1, 128), 1) < 64
    for p in range(NS // 2):
        a = slot_order[:, p * 128 : (p + 1) * 128]
        b = slot_cluster[:, p * 128 : (p + 1) * 128]
        meta_out[2 * p] = jnp.where(low, a, pltpu.roll(b, 64, 1))
        meta_out[2 * p + 1] = jnp.where(low, pltpu.roll(a, 64, 1), b)
    for k in SPLITS:
        if k:
            remote(meta_out.at[k], meta_mid.at[k], ma_s, ma_r, (me_o, split_at(k))).start()
    meta_mid[0] = meta_out[0]

    fill(0)
    for b in STEPS[0:4]:
        if b:
            pl.semaphore_wait(ready.at[b], 1)
        for k in SPLITS:
            ship(b, k)

    fill(4)
    for b in STEPS[4:FIRST]:
        pl.semaphore_wait(ready.at[b], 1)
        for k in SPLITS:
            ship(b, k)
    fill(8)
    fill(12)
    for b in STEPS[FIRST:]:
        pl.semaphore_wait(ready.at[b], 1)

    wide, thin = pl.ds(POOL, POOLED - POOL), pl.ds(1, NZ - 1)
    pools = remote(pool_out.at[wide], pool_in.at[wide], po_s, po_r, (me_o, split_at(1)))
    names = remote(id_out.at[thin], id_in.at[thin], id_s, id_r, (me_o, split_at(1)))
    names.wait_recv()
    part = iota((1, 128), 1) // POOL
    ids = []
    for half in range(POOLED // 128):
        lane_ids = id_in[half * 4]
        for k in range(1, 4):
            lane_ids = jnp.where(part == k, id_in[half * 4 + k], lane_ids)
        ids.append(lane_ids)
    ids = jnp.concatenate(ids, axis=1).astype(jnp.int32)
    choose = ones_where(ids == iota((BLOCKS * TAIL, POOLED), 0))
    pools.wait_recv()
    tail_out[...] = dot(choose, pool_in[...], (1, 0)).astype(BF16)

    some = remote(meta_out.at[pl.ds(1, NS - 1)], meta_mid.at[pl.ds(1, NS - 1)], ma_s, ma_r, (me_o, split_at(1)))
    some.wait_recv()
    for k in STEPS[1:]:
        remote(meta_mid, meta_in.at[k], mb_s, mb_r, (owner_at(k), me_s)).start()
    meta_in[0] = meta_mid[...]
    some.wait_send()
    rest = [(b, k) for b in STEPS[FIRST:] for k in SPLITS]
    blocks = [b * NC + kc for b in STEPS for kc in range(NC)]
    for n, k in enumerate(blocks):
        ship_tail(k)
        for pair in rest[n * 3 : (n + 1) * 3]:
            ship(*pair)
    for pair in rest[BLOCKS * 3 :]:
        ship(*pair)

    many = remote(meta_in.at[pl.ds(1, NO - 1)], meta_in.at[pl.ds(1, NO - 1)], mb_s, mb_r, (owner_at(1), me_s))
    many.wait_recv()
    widest = jnp.full((NS, 128), -1.0, F32)
    for i, b in enumerate(STEPS):
        lines = meta_in[b].reshape(NS, 128)
        widest = jnp.maximum(widest, lines)
        for r in range(CAP):
            lane = b * CAP + r
            turned = pltpu.roll(lines, 128 - lane, 1) if lane else lines
            if r < NEAR:
                at = i * PAIR + r * NS + (BLOCKS * TAIL if i >= EARLY else 0)
                meta_col[at : at + NS] = turned
            else:
                for kc in range(NC):
                    at = POOL_AT + (b * NC + kc) * TAIL + (r - NEAR) * NZ
                    meta_col[at : at + NZ] = turned[kc * NZ : (kc + 1) * NZ]
    many.wait_send()
    widest = jnp.max(jnp.max(widest, axis=1, keepdims=True), axis=0, keepdims=True)
    turned = meta_col[...].T
    row_order, row_cluster = turned[0:1], turned[64:65]
    col_order[...] = jnp.broadcast_to(meta_col[:, 0:1], (SLOTS, 128))
    col_cluster[...] = jnp.broadcast_to(meta_col[:, 64:65], (SLOTS, 128))


    def take(i):
        b = STEPS[i]
        first = LEAF if b == 0 else 0
        span = pl.ds(b * BLOCK + first, BLOCK - first)
        remote(
            send.at[span], recv.at[span], send_sem.at[b], recv_sem.at[b], (me_o, split_at(1))
        ).wait_recv()
        woven = dot(unweave, recv[b * BLOCK : (b + 1) * BLOCK], (1, 0)).astype(BF16)
        at = i * PAIR + (BLOCKS * TAIL if i >= EARLY else 0)
        for q in range(8):
            keys[at : at + PAIR, q * EIGHTH : (q + 1) * EIGHTH] = woven[q * PAIR : (q + 1) * PAIR]

    def grade(lo, hi):
        scores = dot(keys[0:hi], keys[lo:hi], (1, 1))
        for at in range(lo, hi, 128):
            span = slice(at, at + 128)
            new_order, new_cluster = row_order[:, span], row_cluster[:, span]
            score = jnp.where(col_cluster[0:hi] == new_cluster, scores[:, at - lo : at - lo + 128], -1.0)
            earlier = col_order[0:hi] < new_order
            best_row[:, span] = jnp.max(jnp.where(earlier, score, -1.0), axis=0, keepdims=True)
            later = new_order < col_order[0:hi]
            best_col[0:hi] = jnp.maximum(best_col[0:hi], jnp.where(later, score, -1.0))

    best_col[...] = jnp.full((SLOTS, 128), -1.0, F32)
    for i in range(8):
        take(i)
    grade(0, 8 * PAIR)
    for i in range(8, EARLY):
        take(i)
    grade(8 * PAIR, POOL_AT)
    span = pl.ds(POOL_AT + TAIL, (BLOCKS - 1) * TAIL)
    tails = remote(
        tail_out.at[pl.ds(TAIL, (BLOCKS - 1) * TAIL)], keys.at[span], ta_s, ta_r, (me_o, split_at(1))
    )
    tails.wait_recv()
    grade(POOL_AT, POOL_AT + 256)
    grade(POOL_AT + 256, POOL_AT + 512)
    for i in range(EARLY, NO):
        take(i)
    grade(POOL_AT + 512, SLOTS)

    final = jnp.max(best_col[...], axis=1, keepdims=True)
    final = jnp.maximum(final, jnp.broadcast_to(best_row[...], (128, SLOTS)).T)
    lanes = iota((NZ, 128), 1)
    for i, b in enumerate(STEPS):
        stay = jnp.zeros((NZ, 128), F32)
        leave = jnp.zeros((NZ, 128), F32)
        for r in range(CAP):
            if r < NEAR:
                at = i * PAIR + r * NS + (BLOCKS * TAIL if i >= EARLY else 0)
                gap = NZ
            else:
                at = POOL_AT + b * NC * TAIL + (r - NEAR) * NZ
                gap = TAIL
            stay = jnp.where(lanes == r, final[at : at + NZ], stay)
            leave = jnp.where(lanes == CAP + r, final[at + gap : at + gap + NZ], leave)
        swap_out[b * NZ : (b + 1) * NZ] = leave
        best_col[b * NZ : (b + 1) * NZ] = stay
    swap = remote(swap_out, swap_in, sw_s, sw_r, (me_o, split_at(NZ)))
    swap.start()
    for n, k in enumerate(FAR):
        far_out[n] = best_col[k : k + 1]
        far_out[len(FAR) + n] = swap_out[k : k + 1]
    for n, k in enumerate(FAR):
        ko, dz = k // NZ, k % NZ
        remote(
            far_out.at[n], ans_in.at[k], fa_s, an_r, (owner_at(ko, -1), split_at(dz, -1))
        ).start()
        remote(
            far_out.at[len(FAR) + n], far_in.at[n], fa_s, fa_r, (owner_at(ko, -1), split_at(NZ + dz, -1))
        ).start()
    swap.wait_recv()
    both = best_col[0:CHIPS] + swap_in[...]
    ans_out[...] = both.reshape(CHIPS, 1, 128)
    for k in WAYS[len(FAR) :]:
        remote(
            ans_out.at[k], ans_in.at[k], an_s, an_r, (owner_at(k // NZ, -1), split_at(k % NZ, -1))
        ).start()
    ans_in[0] = ans_out[0]
    swap.wait_send()
    tails.wait_send()
    pools.wait_send()
    names.wait_send()
    for b in range(NO):
        first = LEAF if b == 0 else 0
        span = pl.ds(b * BLOCK + first, BLOCK - first)
        remote(
            send.at[span], recv.at[span], send_sem.at[b], recv_sem.at[b], (me_o, split_at(1))
        ).wait_send()
    most, less = pl.ds(1, CHIPS - 1), pl.ds(1, CHIPS - 1 - len(FAR))
    remote(ans_out.at[less], ans_in.at[less], an_s, an_r, (me_o, split_at(1))).wait_send()
    alone = pl.ds(0, len(FAR))
    remote(far_out, far_out, fa_s, fa_r, (me_o, split_at(1))).wait_send()
    remote(ans_out.at[most], ans_in.at[most], an_s, an_r, (me_o, split_at(1))).wait_recv()
    remote(far_out.at[alone], far_in.at[alone], fa_s, fa_r, (me_o, split_at(1))).wait_recv()
    for n, k in enumerate(FAR):
        ans_in[k] = ans_in[k] + far_in[n]

    table = ans_in[...].reshape(CHIPS, 128).T[0:8]
    high = table.astype(BF16)
    rest = table - high.astype(F32)
    mid = rest.astype(BF16)
    tiny = (rest - mid.astype(F32)).astype(BF16)
    mine = dot(high, onehot[...], (1, 0)) + dot(mid, onehot[...], (1, 0)) + dot(tiny, onehot[...], (1, 0))
    mine = jnp.sum(jnp.where(line == rel_c * CAP + rank, mine, 0.0), axis=0, keepdims=True)
    out_ref[...] = jnp.where(widest >= FLAG, REDO, mine)


def common(rows, width):
    return [
        pltpu.VMEM((CHIPS, ROWS), BF16),
        pltpu.VMEM((1, ROWS), jnp.int32),
        pltpu.VMEM((rows, width), BF16),
        pltpu.VMEM((rows, width), BF16),
        pltpu.VMEM((SLOTS, DIM), BF16),
        pltpu.VMEM((NS, 1, 128), F32),
        pltpu.VMEM((NS, 1, 128), F32),
        pltpu.VMEM((NO, NS, 1, 128), F32),
        pltpu.VMEM((SLOTS, 128), F32),
        pltpu.VMEM((SLOTS, 128), F32),
        pltpu.VMEM((1, SLOTS), F32),
        pltpu.VMEM((CHIPS, 128), F32),
        pltpu.VMEM((CHIPS, 128), F32),
        pltpu.VMEM((CHIPS, 1, 128), F32),
        pltpu.VMEM((CHIPS, 1, 128), F32),
    ]


def call(kernel, name, number, out, small, scratch, args):
    hbm = pl.BlockSpec(memory_space=pltpu.HBM)
    vmem = pl.BlockSpec(memory_space=pltpu.VMEM)
    return pl.pallas_call(
        kernel,
        name=name,
        out_shape=out,
        in_specs=[hbm] + [vmem if small else hbm] * 2,
        out_specs=vmem,
        scratch_shapes=scratch,
        compiler_params=pltpu.CompilerParams(
            collective_id=number, has_side_effects=True, vmem_limit_bytes=56 << 20
        ),
        cost_estimate=pl.CostEstimate(
            flops=8 << 30, bytes_accessed=4 << 20, transcendentals=SLOTS
        ),
    )(*args)


def local(embeddings, cluster_id, doc_order):
    args = (embeddings, cluster_id.reshape(1, ROWS), doc_order.reshape(1, ROWS))
    dma = pltpu.SemaphoreType.DMA
    ready = pltpu.SemaphoreType.REGULAR((NO,))
    result = jax.ShapeDtypeStruct((1, ROWS), F32)
    pooled_scratch = [pltpu.VMEM((ROWS, DIM), BF16)] + common(NO * BLOCK, EIGHTH) + [
        pltpu.VMEM((POOLED, DIM), BF16),
        pltpu.VMEM((POOLED, DIM), BF16),
        pltpu.VMEM((NZ, 1, 128), F32),
        pltpu.VMEM((NZ, 1, 128), F32),
        pltpu.VMEM((BLOCKS * TAIL, DIM), BF16),
        pltpu.VMEM((SLOTS, 128), F32),
        pltpu.VMEM((SLOTS, 128), F32),
        pltpu.VMEM((2 * len(FAR), 1, 128), F32),
        pltpu.VMEM((len(FAR), 1, 128), F32),
        dma, dma((NO,)), dma((NO,)),
        *[dma] * 16,
        ready,
    ]
    line = pltpu.VMEM((1, ROWS), jnp.int32)
    full_scratch = [pltpu.VMEM((ROWS, DIM), BF16), line, line] + common(NO * BLOCK, QUART) + [
        dma((3,)), dma((NO,)), dma((NO,)),
        *[dma] * 8,
        ready,
    ]
    best = call(pooled_kernel, "pooled", 0, result, True, pooled_scratch, args)

    def again(args, best):
        return call(full_kernel, "full", 1, result, False, full_scratch, args)

    def keep(args, best):
        return best

    return lax.cond(best[0, 0] > REDO / 2, again, keep, args, best).reshape(ROWS)


def solution(mesh):
    in_specs = (P(("owner", "split"), None), P(("owner", "split")), P(("owner", "split")))
    out_specs = P(("owner", "split"))
    return jax.shard_map(local, mesh=mesh, in_specs=in_specs, out_specs=out_specs, check_vma=False)
```
